128 devices in a mesh: visit: 4 (over z), sky: 32 (over y, x, core).
Axes of the slice: x: 4, y: 4, z: 4, core: 2. Of those that a mesh axis runs over, the one named last changes fastest.
Arguments:
- exposure: bfloat16 [4, 4096, 4096], P('visit', 'sky'), may hold values from -6 to 6
- variance: bfloat16 [4, 4096, 4096], P('visit', 'sky'), may hold values from 0.5 to 8
- pixel_mask: int32 [4, 4096, 4096], P('visit', 'sky'), may hold values 0 or 1
- psf_kernel: bfloat16 [4, 2, 21], P('visit'), may hold values from 0.049804688 to 0.19921875
- block_owner: int32 [4, 32, 32], P('visit', 'sky'), may hold values from 0 to 31, as said below
- patch_index: int32 [4, 32, 32, 4], P('visit', 'sky'), may hold values from 0 to 31
- pair_stretch: bfloat16 [4, 32, 32, 4, 2], P('visit', 'sky'), may hold values from -0.019897461 to 0.019897461
- pair_offset: bfloat16 [4, 32, 32, 4, 2], P('visit', 'sky'), may hold values from -1.5 to 1.5
Outputs:
- coadd_image: float32 [1024, 128, 128], P(('visit', 'sky'))
The draws below stay inside these ranges and needn't reach their ends.
Inputs may be any that keep to these rules, and one draw needn't show every extreme that they name: `block_owner`: among the 32 blocks of one device, at most 2 name the same owner; in every draw one owner is named by exactly 2 blocks of every device.
All inputs are finite; a program needn't handle non-finite values. No bound on the sum of `pixel_mask` on one device may be relied on, other than what follows from the above.
Results may differ from the reference program's by a relative error of at most 0.007.
Values may be sent and summed in bfloat16 or wider, within the bound.
No kernel may reach another device: no remote copies, remote signals or barrier semaphores. Data moves between devices by JAX's collectives and lax.ppermute only.
A program may use at most 128 MiB of HBM per device.

```python
import math
import jax
import jax.numpy as jnp
import numpy as np
from jax import lax

BS = 128
CCD_COLS = 4096
PAIRS = 4
VIS_DEV = 1
PB_DEV = 8
GROUPS = 4
OWNERS = 32
TAPS = 21
VISITS = 4
CCD_ROWS = 4096
COLBLK = 32
BLK_DEV = 32
CAP = 2
PB_OWN = 32
PATCH_BLKS = 1024
N_VISIT = 4
N_SKY = 32


def draw_block_owner(key, part):
    key = jax.random.fold_in(key, 11)
    chosen_key, heat_key, device_key = jax.random.split(key, 3)
    preferred_owner = jax.random.randint(chosen_key, (), 0, OWNERS)
    load_level = jax.random.randint(heat_key, (OWNERS,), 0, 4)
    entry_list = jnp.arange(OWNERS * CAP, dtype=jnp.int32)
    entry_holder = entry_list // CAP
    extra_score = load_level[entry_holder] * 65536 + jnp.where(entry_holder == preferred_owner, 524288, 0)

    def one_device(device_sub):
        pick_key, order_key = jax.random.split(device_sub)
        random_jitter = jax.random.randint(pick_key, (OWNERS * CAP,), 0, 262144)
        owner_scores = (random_jitter + extra_score) * 1024 + entry_list
        top_values, picked = lax.top_k(owner_scores, BLK_DEV)
        return jax.random.permutation(order_key, entry_holder[picked])
    device_keys = jax.random.split(device_key, GROUPS * OWNERS)
    return jax.vmap(one_device)(device_keys).reshape(GROUPS, OWNERS, BLK_DEV).astype(jnp.int32)


def set_ends(entries, rng, least, top_value):
    shape = entries.shape
    spot = [jax.random.randint(jax.random.fold_in(rng, axis), (), 0, shape[axis]) for axis in range(len(shape))]
    entries = entries.at[tuple(spot)].set(least)
    longest = shape.index(max(shape))
    spot[longest] = (spot[longest] + 1) % shape[longest]
    return entries.at[tuple(spot)].set(top_value)


def block_levels(own_key, shape, cuts, smallest, top_value):
    factor_of, own = 1.0, jax.random.fold_in(own_key, 6)
    for dim, parts in cuts:
        draws = jnp.exp(jax.random.uniform(jax.random.fold_in(own, dim), (parts,), jnp.float32, smallest / len(cuts), top_value / len(cuts)))
        factor_of = factor_of * jnp.repeat(draws, shape[dim] // parts).reshape([-1 if axis == dim else 1 for axis in range(len(shape))])
    return factor_of


def cumulative_ranks(amount, lean):
    portions = [(1 << 20) // math.isqrt(rank ** lean) + 1 for rank in range(1, amount + 1)]
    deviation = 1 + sum(portions) // (1 << 30)
    return np.cumsum(np.array([max(1, weight // deviation) for weight in portions]))


def ranked_ids(key, shape, amount, lean):
    table = cumulative_ranks(amount, lean)
    lot = jax.random.randint(jax.random.fold_in(key, 1), shape, 0, int(table[amount - 1]))
    grade = jnp.searchsorted(jnp.asarray(table, jnp.int32), lot, side="right")
    return jax.random.permutation(jax.random.fold_in(key, 2), amount)[grade].astype(jnp.int32)


def scatter_about(key, extent, width, reach, cuts=(), kind=jnp.bfloat16):
    entries = jax.random.normal(key, extent, jnp.float32) * width
    if len(cuts) > 0:
        entries = block_levels(key, extent, cuts, -0.22, 0.18) * entries
    return jnp.clip(entries, min=-reach, max=reach).astype(kind)


def setup_inputs(seed: int = 0) -> dict:
    key_list = jax.random.split(jax.random.key(seed), 9)
    return {
        "exposure": scatter_about(key_list[0], (VISITS, CCD_ROWS, CCD_COLS), 1.0, 6.0, ((0, 4), (1, 32))),
        "variance": jnp.clip(jnp.exp(math.log(8.0) - 2.7725887 * jax.random.uniform(key_list[1], (VISITS, CCD_ROWS, CCD_COLS), jnp.float32) ** block_levels(key_list[1], (VISITS, CCD_ROWS, CCD_COLS), ((0, 4), (1, 32)), -0.2, 0.2)), 0.5, 8.0).astype(jnp.bfloat16),
        "pixel_mask": set_ends((jax.random.randint(key_list[2], (VISITS, CCD_ROWS, CCD_COLS), 0, 8) < 7).astype(jnp.int32), jax.random.fold_in(key_list[2], 1), 0, 1),
        "psf_kernel": jnp.clip(0.049804688 + 0.14941406 * jax.random.uniform(key_list[3], (VISITS, 2, TAPS), jnp.float32) ** block_levels(key_list[3], (VISITS, 2, TAPS), ((0, 4),), -0.2, 0.2), 0.049804688, 0.19921875).astype(jnp.bfloat16),
        "block_owner": draw_block_owner(jax.random.fold_in(key_list[8], 71), 0),
        "patch_index": set_ends(ranked_ids(key_list[5], (GROUPS, OWNERS, BLK_DEV, PAIRS), PB_OWN, 2), jax.random.fold_in(key_list[5], 3), 0, PB_OWN - 1).astype(jnp.int32),
        "pair_stretch": jnp.clip(jax.random.uniform(key_list[6], (GROUPS, OWNERS, BLK_DEV, PAIRS, 2), jnp.float32, -0.019897461, 0.019897461) * block_levels(key_list[6], (GROUPS, OWNERS, BLK_DEV, PAIRS, 2), ((0, 4), (1, 32)), -0.4, 0.0), -0.019897461, 0.019897461).astype(jnp.bfloat16),
        "pair_offset": jnp.clip(jax.random.uniform(key_list[7], (GROUPS, OWNERS, BLK_DEV, PAIRS, 2), jnp.float32, -1.5, 1.5) * block_levels(key_list[7], (GROUPS, OWNERS, BLK_DEV, PAIRS, 2), ((0, 4), (1, 32)), -0.4, 0.0), -1.5, 1.5).astype(jnp.bfloat16),
    }


WINDOW = 3.0


def lanczos_maps(stretch, offset, block_side):
    pixels = jnp.arange(block_side).astype(jnp.float32)
    centre = (block_side - 1) / 2.0
    source = (1.0 + stretch.astype(jnp.float32))[..., None] * (pixels - centre) + centre + offset.astype(jnp.float32)[..., None]
    spread = source[..., :, None] - pixels
    inside = jnp.abs(spread) < WINDOW
    kernel = jnp.sinc(spread) * jnp.sinc(spread / WINDOW)
    return jnp.where(inside, kernel, jnp.zeros_like(kernel)).astype(jnp.bfloat16)


def warp_blocks(planes, maps):
    half_warp = jnp.einsum("npij,ncjk->npcik", maps[:, :, 0].astype(jnp.float32), planes.astype(jnp.float32)).astype(jnp.bfloat16)
    return jnp.einsum("npcij,npkj->npcik", half_warp.astype(jnp.float32), maps[:, :, 1].astype(jnp.float32)).astype(jnp.bfloat16)


def shifted_sum(surface, tap_values, axis):
    tap_count = tap_values.shape[-1]
    kernel_half = (tap_count - 1) // 2
    widths = [(0, 0), (0, 0), (0, 0)]
    widths[axis] = (kernel_half, kernel_half)
    padded = jnp.pad(surface, widths)
    length = surface.shape[axis]
    summed = jnp.zeros_like(surface)
    for lag_index in range(tap_count):
        shifted = lax.slice_in_dim(padded, lag_index, lag_index + length, axis=axis)
        summed = summed + tap_values[:, lag_index][:, None, None] * shifted
    return summed


def rounded(values):
    return lax.optimization_barrier(values.astype(jnp.bfloat16)).astype(jnp.float32)


def reference(exposure, variance, pixel_mask, psf_kernel, block_owner, patch_index, pair_stretch, pair_offset):
    accum = jnp.zeros((PATCH_BLKS, 2, BS, BS), jnp.float32)

    def group_step(accum, group):
        start = group * VIS_DEV
        images = lax.dynamic_slice_in_dim(exposure, start, VIS_DEV, 0).astype(jnp.float32)
        noises = lax.dynamic_slice_in_dim(variance, start, VIS_DEV, 0).astype(jnp.float32)
        usable = lax.dynamic_slice_in_dim(pixel_mask, start, VIS_DEV, 0).astype(jnp.float32)
        kernels = lax.dynamic_slice_in_dim(psf_kernel, start, VIS_DEV, 0).astype(jnp.float32)
        across = kernels[:, 0]
        vertical = kernels[:, 1]
        across_square = rounded(across * across)
        down_square = rounded(vertical * vertical)
        row_pass = rounded(shifted_sum(images, across, 2))
        var_pass = rounded(shifted_sum(noises, across_square, 2))
        matched = shifted_sum(row_pass, vertical, 1)
        matched_var = shifted_sum(var_pass, down_square, 1)
        weight_plane = usable / matched_var
        weighted = (weight_plane * matched).astype(jnp.bfloat16)
        planes = jnp.stack([weighted, weight_plane.astype(jnp.bfloat16)], axis=1)
        planes = planes.reshape(VIS_DEV, 2, N_SKY, BS, COLBLK, BS)
        planes = planes.transpose(2, 0, 4, 1, 3, 5).reshape(N_SKY, BLK_DEV, 2, BS, BS)
        owners = lax.dynamic_index_in_dim(block_owner, group, 0, keepdims=False)
        targets = lax.dynamic_index_in_dim(patch_index, group, 0, keepdims=False)
        stretches = lax.dynamic_index_in_dim(pair_stretch, group, 0, keepdims=False)
        offsets = lax.dynamic_index_in_dim(pair_offset, group, 0, keepdims=False)

        def sky_step(accum, pieces):
            blocks, owner_row, target_row, stretch_row, offset_row = pieces
            warped = warp_blocks(blocks, lanczos_maps(stretch_row, offset_row, BS))
            dest = ((target_row // PB_DEV) * N_SKY + owner_row[:, None]) * PB_DEV + target_row % PB_DEV
            accum = accum.at[dest.reshape(-1).astype(jnp.int32)].add(warped.reshape(-1, 2, BS, BS).astype(jnp.float32))
            return accum, None

        accum, unused = lax.scan(sky_step, accum, (planes, owners, targets, stretches, offsets))
        return accum, None

    accum, unused = lax.scan(group_step, accum, jnp.arange(N_VISIT).astype(jnp.int32))
    return accum[:, 0] / jnp.maximum(accum[:, 1], 1.0)
```

```python
import functools
import math

import jax
import jax.numpy as jnp
from jax import lax
from jax.experimental import pallas as pl
from jax.experimental.pallas import tpu as pltpu
from jax.sharding import PartitionSpec as P

BS = 128
HALO = 16
MARGIN = 16
CAP = 2
PB_DEV = 8
PER_STEP = 4
CUTS = (0, 64, 128)
VMEM = 48 * 1024 * 1024


def spans(cuts):
    result = []
    for part in range(len(cuts) - 1):
        first, last = part == 0, part == len(cuts) - 2
        out_from = 0 if first else cuts[part] - MARGIN
        out_to = cuts[-1] if last else cuts[part + 1] - MARGIN
        read_from = 0 if first else out_from - MARGIN
        result.append((cuts[part], cuts[part + 1], read_from, out_from, out_to))
    return result


def band(rows, columns, shift, taps_ref, which, square):
    lag = (
        lax.broadcasted_iota(jnp.int32, (rows, columns), 0)
        - lax.broadcasted_iota(jnp.int32, (rows, columns), 1)
        + shift
    )
    matrix = jnp.zeros((rows, columns), jnp.float32)
    for tap in range(taps_ref.shape[1]):
        value = taps_ref[which, tap]
        matrix = jnp.where(lag == tap, value * value if square else value, matrix)
    return matrix.astype(jnp.bfloat16)


def filter_kernel(cuts, slot_ref, taps_ref, exp_ref, var_ref, mask_ref, top_ref, bottom_ref, *rest):
    outs, framed, across_ref, down_ref = rest[:-3], rest[-3], rest[-2], rest[-1]
    rows, columns = exp_ref.shape
    half = (taps_ref.shape[1] - 1) // 2
    side = jnp.zeros((rows + 2 * HALO, BS), jnp.bfloat16)
    for plane, ref in enumerate((exp_ref, var_ref)):
        framed[plane, :, :BS] = side
        framed[plane, :, BS + columns :] = side
        framed[plane, :HALO, BS : BS + columns] = top_ref[plane]
        framed[plane, HALO : HALO + rows, BS : BS + columns] = ref[...]
        framed[plane, HALO + rows :, BS : BS + columns] = bottom_ref[plane]
        square = plane == 1
        across_ref[plane] = band(4 * BS, 2 * BS, half - BS, taps_ref, 0, square)
        lag = (
            lax.broadcasted_iota(jnp.int32, (rows, rows + 2 * HALO), 1)
            - lax.broadcasted_iota(jnp.int32, (rows, rows + 2 * HALO), 0)
            + half
            - HALO
        )
        matrix = jnp.zeros(lag.shape, jnp.float32)
        for tap in range(taps_ref.shape[1]):
            value = taps_ref[1, tap]
            matrix = jnp.where(lag == tap, value * value if square else value, matrix)
        down_ref[plane] = matrix.astype(jnp.bfloat16)

    @pl.loop(0, columns // (2 * BS))
    def _(tile):
        start = pl.multiple_of(tile * 2 * BS, 2 * BS)
        matched = []
        for plane in range(2):
            passed = jnp.dot(
                framed[plane, :, pl.ds(start, 4 * BS)],
                across_ref[plane],
                preferred_element_type=jnp.float32,
            ).astype(jnp.bfloat16)
            matched.append(jnp.dot(down_ref[plane], passed, preferred_element_type=jnp.float32))
        weight = mask_ref[:, pl.ds(start, 2 * BS)].astype(jnp.float32) / matched[1]
        weighted = (weight * matched[0]).astype(jnp.bfloat16)
        weight = weight.astype(jnp.bfloat16)
        for block in range(2):
            slot = slot_ref[tile * 2 + block]
            lanes = slice(block * BS, (block + 1) * BS)
            for out, lo, hi in zip(outs, cuts[:-1], cuts[1:]):
                out[slot, 0] = weighted[lo:hi, lanes]
                out[slot, 1] = weight[lo:hi, lanes]


def sine_cosine(angle):
    square = angle * angle
    sine = jnp.zeros_like(angle)
    cosine = jnp.zeros_like(angle)
    for term in range(8, -1, -1):
        sine = sine * square + (-1.0) ** term / math.factorial(2 * term + 1)
        cosine = cosine * square + (-1.0) ** term / math.factorial(2 * term)
    return sine * angle, cosine, sine


def map_kernel(shapes, stretch_ref, offset_ref, column_ref, *rest):
    outs, near_ref, taps = rest[:-2], rest[-2], rest[-1]
    step_slots = column_ref.shape[0]
    pixels = lax.broadcasted_iota(jnp.int32, (step_slots * 8, BS), 1).astype(jnp.float32)
    centre = (BS - 1) / 2.0
    source = (1.0 + stretch_ref[...]) * (pixels - centre) + centre + offset_ref[...]
    near = jnp.round(source)
    fraction = source - near
    near_ref[...] = near
    whole, _, whole_sinc = sine_cosine(math.pi * fraction)
    third, third_cos, third_sinc = sine_cosine((math.pi / 3.0) * fraction)
    for k in range(-3, 4):
        if k == 0:
            value = whole_sinc * third_sinc
        else:
            x = fraction - k
            sign = -1.0 if k % 2 else 1.0
            angle = math.pi * k / 3.0
            slow = third * math.cos(angle) - third_cos * math.sin(angle)
            value = (sign * 3.0 / math.pi**2) * whole * slow / (x * x)
            value = jnp.where(jnp.abs(x) < 3.0, value, 0.0)
        taps[k + 3] = value
    rows = lax.broadcasted_iota(jnp.int32, (BS, BS), 0).astype(jnp.float32)

    @pl.loop(0, step_slots)
    def _(slot):
        base = pl.multiple_of(slot * 8, 8)
        near_slot = near_ref[pl.ds(base, 8), :]
        taps_slot = [taps[k, pl.ds(base, 8), :] for k in range(7)]
        for pair in range(4):
            for direction in range(2):
                row = pair * 2 + direction
                lag = rows - near_slot[row : row + 1, :]
                matrix = jnp.zeros((BS, BS), jnp.float32)
                for k in range(7):
                    matrix = jnp.where(lag == float(k - 3), taps_slot[k][row : row + 1, :], matrix)
                if direction == 1:
                    column_ref[slot, :, pair * BS : (pair + 1) * BS] = matrix.astype(jnp.bfloat16)
                else:
                    turned = matrix.T.astype(jnp.bfloat16)
                    for out, (_, to, read_from, out_from, out_to) in zip(outs, shapes):
                        piece = turned[out_from:out_to, :]
                        if read_from:
                            piece = matrix[read_from:, :].T[out_from:out_to, :].astype(jnp.bfloat16)
                        out[slot, pair, :, : to - read_from] = piece[:, : to - read_from]


def warp_kernel(span, before, aim_ref, *refs):
    cut_from, cut_to, read_from, out_from, out_to = span
    count = len(before) + 1
    blocks, column_ref, row_ref = refs[:count], refs[count], refs[count + 1]
    outs, total = refs[count + 2 : -1], refs[-1]
    step = pl.program_id(0)

    @pl.when(step == 0)
    def _():
        total[...] = jnp.zeros_like(total)

    depth = cut_to - read_from
    for slot in range(PER_STEP):
        pieces = [ref[slot] for ref in blocks]
        planes = jnp.concatenate(
            [piece[plane] for plane in range(2) for piece in pieces], axis=0
        )
        half_warp = jnp.dot(planes, column_ref[slot], preferred_element_type=jnp.float32).astype(
            jnp.bfloat16
        )
        for pair in range(4):
            lanes = slice(pair * BS, (pair + 1) * BS)
            both = jnp.concatenate([half_warp[:depth, lanes], half_warp[depth:, lanes]], axis=1)
            aim = aim_ref[(step * PER_STEP + slot) * 4 + pair]
            total[aim] += jnp.dot(
                row_ref[slot, pair, :, :depth], both, preferred_element_type=jnp.float32
            )

    @pl.when(step == pl.num_programs(0) - 1)
    def _():
        for index, out in enumerate(outs):
            out[...] = total[index * PB_DEV : (index + 1) * PB_DEV].astype(out.dtype)


def local(
    exposure, variance, pixel_mask, psf_kernel, block_owner, patch_index, pair_stretch, pair_offset
):
    shapes = spans(CUTS)
    _, rows, columns = exposure.shape
    block_count = columns // BS
    owners = lax.axis_size("sky")
    groups = lax.axis_size("visit")
    slots = owners * CAP
    pairs = patch_index.shape[-1]
    params = pltpu.CompilerParams(vmem_limit_bytes=VMEM)
    smem = pl.BlockSpec(memory_space=pltpu.SMEM)
    vmem = pl.BlockSpec(memory_space=pltpu.VMEM)

    low = jnp.concatenate([exposure[:, rows - HALO :], variance[:, rows - HALO :]], axis=0)
    high = jnp.concatenate([exposure[:, :HALO], variance[:, :HALO]], axis=0)
    top = lax.ppermute(low, "sky", [(i, i + 1) for i in range(owners - 1)])
    bottom = lax.ppermute(high, "sky", [(i + 1, i) for i in range(owners - 1)])

    owner = block_owner.reshape(block_count)
    order = jnp.arange(block_count)
    rank = jnp.sum((owner[:, None] == owner[None, :]) & (order[None, :] < order[:, None]), axis=1)
    slot = (owner * CAP + rank).astype(jnp.int32)
    claimed = (slot[None, :] == jnp.arange(slots)[:, None]).astype(jnp.bfloat16)
    facts = jnp.concatenate(
        [
            pair_stretch.reshape(block_count, 2 * pairs),
            pair_offset.reshape(block_count, 2 * pairs),
            patch_index.reshape(block_count, pairs).astype(jnp.bfloat16),
            jnp.ones((block_count, 1), jnp.bfloat16),
        ],
        axis=1,
    )
    table = jnp.dot(claimed, facts, preferred_element_type=jnp.float32).astype(jnp.bfloat16)

    planes = pl.pallas_call(
        functools.partial(filter_kernel, CUTS),
        out_shape=[
            jax.ShapeDtypeStruct((slots, 2, hi - lo, BS), jnp.bfloat16)
            for lo, hi in zip(CUTS[:-1], CUTS[1:])
        ],
        in_specs=[smem, smem] + [vmem] * 5,
        out_specs=[vmem] * len(shapes),
        scratch_shapes=[
            pltpu.VMEM((2, rows + 2 * HALO, columns + 2 * BS), jnp.bfloat16),
            pltpu.VMEM((2, 4 * BS, 2 * BS), jnp.bfloat16),
            pltpu.VMEM((2, rows, rows + 2 * HALO), jnp.bfloat16),
        ],
        compiler_params=params,
        name="filter",
    )(
        slot,
        psf_kernel.reshape(2, -1).astype(jnp.float32),
        exposure.reshape(rows, columns),
        variance.reshape(rows, columns),
        pixel_mask.reshape(rows, columns),
        top,
        bottom,
    )

    def exchange(array):
        return lax.all_to_all(array, "sky", split_axis=0, concat_axis=0, tiled=True)

    arrived = [exchange(part) for part in planes]
    known = exchange(table).astype(jnp.float32)

    map_slots = 16
    maps = pl.pallas_call(
        functools.partial(map_kernel, shapes),
        grid=(slots // map_slots,),
        out_shape=[jax.ShapeDtypeStruct((slots, BS, pairs * BS), jnp.bfloat16)]
        + [
            jax.ShapeDtypeStruct((slots, pairs, out_to - out_from, BS), jnp.bfloat16)
            for _, _, _, out_from, out_to in shapes
        ],
        in_specs=[pl.BlockSpec((map_slots * 2 * pairs, 1), lambda i: (i, 0))] * 2,
        out_specs=[pl.BlockSpec((map_slots, BS, pairs * BS), lambda i: (i, 0, 0))]
        + [
            pl.BlockSpec((map_slots, pairs, out_to - out_from, BS), lambda i: (i, 0, 0, 0))
            for _, _, _, out_from, out_to in shapes
        ],
        scratch_shapes=[
            pltpu.VMEM((map_slots * 2 * pairs, BS), jnp.float32),
            pltpu.VMEM((7, map_slots * 2 * pairs, BS), jnp.float32),
        ],
        compiler_params=params,
        name="maps",
    )(
        known[:, : 2 * pairs].reshape(slots * 2 * pairs, 1),
        known[:, 2 * pairs : 4 * pairs].reshape(slots * 2 * pairs, 1),
    )
    column_maps, row_maps = maps[0], maps[1:]

    patch = known[:, 4 * pairs : 5 * pairs].astype(jnp.int32)
    distance = (patch // PB_DEV - lax.axis_index("visit")) % groups
    aims = jnp.where(
        known[:, 5 * pairs :] > 0.5, distance * PB_DEV + patch % PB_DEV, groups * PB_DEV
    )
    aims = aims.reshape(slots * pairs)

    results = []
    for part, span in enumerate(shapes):
        cut_from, cut_to, read_from, out_from, out_to = span
        before = [arrived[part - 1]] if part else []
        height = out_to - out_from
        specs = []
        if part:
            reach = cut_from - read_from
            last = (cut_from - shapes[part - 1][0]) // reach - 1
            specs.append(
                pl.BlockSpec((PER_STEP, 2, reach, BS), functools.partial(lambda q, i, _: (i, 0, q, 0), last))
            )
        specs.append(pl.BlockSpec((PER_STEP, 2, cut_to - cut_from, BS), lambda i, _: (i, 0, 0, 0)))
        specs.append(pl.BlockSpec((PER_STEP, BS, pairs * BS), lambda i, _: (i, 0, 0)))
        specs.append(pl.BlockSpec((PER_STEP, pairs, height, BS), lambda i, _: (i, 0, 0, 0)))
        sums = pl.pallas_call(
            functools.partial(warp_kernel, span, before),
            grid_spec=pltpu.PrefetchScalarGridSpec(
                num_scalar_prefetch=1,
                grid=(slots // PER_STEP,),
                in_specs=specs,
                out_specs=[pl.BlockSpec((PB_DEV, height, 2 * BS), lambda i, _: (0, 0, 0))] * groups,
                scratch_shapes=[pltpu.VMEM((groups * PB_DEV + 1, height, 2 * BS), jnp.float32)],
            ),
            out_shape=[
                jax.ShapeDtypeStruct(
                    (PB_DEV, height, 2 * BS), jnp.float32 if index == 0 else jnp.bfloat16
                )
                for index in range(groups)
            ],
            compiler_params=params,
            name="warp",
        )(aims, *before, arrived[part], column_maps, row_maps[part])
        whole = sums[0]
        for step in range(1, groups):
            whole = whole + lax.ppermute(
                sums[step], "visit", [(i, (i + step) % groups) for i in range(groups)]
            ).astype(jnp.float32)
        results.append(whole[:, :, :BS] / jnp.maximum(whole[:, :, BS:], 1.0))
    return jnp.concatenate(results, axis=1)


def solution(mesh):
    return jax.shard_map(
        local,
        mesh=mesh,
        in_specs=(
            P("visit", "sky", None),
            P("visit", "sky", None),
            P("visit", "sky", None),
            P("visit", None, None),
            P("visit", "sky", None),
            P("visit", "sky", None, None),
            P("visit", "sky", None, None, None),
            P("visit", "sky", None, None, None),
        ),
        out_specs=P(("visit", "sky"), None, None),
        check_vma=False,
    )
```

```python
import functools
import math

import jax
import jax.numpy as jnp
from jax import lax
from jax.experimental import pallas as pl
from jax.experimental.pallas import tpu as pltpu
from jax.sharding import PartitionSpec as P

BS = 128
HALO = 16
BAND = 16
CAP = 2
PB_DEV = 8
CUT = 80
EDGE = CUT - 16
FILTER_COLUMNS = 1024
MAP_SLOTS = 16
WARP_SLOTS = 16
VMEM = 60 * 1024 * 1024


def toeplitz(rows, columns, shift, tap):
    lag = lax.broadcasted_iota(jnp.int32, (rows, columns), 0) - lax.broadcasted_iota(jnp.int32, (rows, columns), 1) + shift
    matrix = jnp.zeros((rows, columns), jnp.float32)
    for index, value in enumerate(tap):
        matrix = jnp.where(lag == index, value, matrix)
    return matrix.astype(jnp.bfloat16)

def filter_kernel(first, last, slot_ref, taps_ref, *refs):
    images, mask_ref, halo_ref = (refs[0:3], refs[3:6]), refs[6], refs[7]
    out, framed, across_ref, down_ref = refs[8:]
    rows, columns = mask_ref.shape
    height = last - first
    tall = height + 2 * HALO
    wide = 2 * BS
    half = (taps_ref.shape[-1] - 1) // 2
    step, steps = pl.program_id(0), pl.num_programs(0)

    @pl.when(step == 0)
    def _():
        empty = jnp.zeros((BS, BS), jnp.bfloat16)
        values = taps_ref[0].astype(jnp.float32)
        for plane in range(2):
            taps = [
                [values[way : way + 1, tap : tap + 1] for tap in range(taps_ref.shape[-1])]
                for way in range(2)
            ]
            if plane == 1:
                taps = [[tap * tap for tap in way] for way in taps]
            left, middle, right = (toeplitz(BS, BS, half + by * BS, taps[0]) for by in (-1, 0, 1))
            pattern = ((left, empty), (middle, left), (right, middle), (empty, right))
            for row, blocks in enumerate(pattern):
                across_ref[plane, row * BS : (row + 1) * BS, :BS] = blocks[0]
                across_ref[plane, row * BS : (row + 1) * BS, BS:] = blocks[1]
            down_ref[plane] = toeplitz(height, tall, half + HALO, taps[1][::-1])

    start = pl.multiple_of(step * columns, columns)
    before = pl.multiple_of(jnp.maximum(start - BS, 0), BS)
    after = pl.multiple_of(jnp.minimum(start + columns, (steps - 1) * columns - BS + columns), BS)
    for plane, parts in enumerate(images):
        halo = [
            halo_ref[plane, :, pl.ds(before, BS)],
            halo_ref[plane, :, pl.ds(start, columns)],
            halo_ref[plane, :, pl.ds(after, BS)],
        ]
        if first == 0:
            strips = ((0, halo), (HALO, [part[: last + HALO, :] for part in parts]))
        else:
            strips = (
                (0, [part[first - HALO :, :] for part in parts]),
                (rows - first + HALO, halo),
            )
        for row, pieces in strips:
            column = 0
            for piece, kept in zip(pieces, (step > 0, None, step < steps - 1)):
                if kept is not None:
                    piece = jnp.where(kept, piece, jnp.zeros_like(piece))
                framed[
                    plane, row : row + piece.shape[0], column : column + piece.shape[1]
                ] = piece
                column += piece.shape[1]

    tiles = columns // wide
    matched = []
    for plane in range(2):
        stack = jnp.concatenate(
            [framed[plane, :, tile * wide : tile * wide + 4 * BS] for tile in range(tiles)], axis=0
        )
        passed = jnp.dot(stack, across_ref[plane], preferred_element_type=jnp.float32).astype(
            jnp.bfloat16
        )
        matched.append(
            [
                jnp.dot(
                    down_ref[plane],
                    passed[tile * tall : (tile + 1) * tall],
                    preferred_element_type=jnp.float32,
                )
                for tile in range(tiles)
            ]
        )
    for tile in range(tiles):
        usable = mask_ref[first:last, tile * wide : (tile + 1) * wide].astype(jnp.float32)
        weight = usable / matched[1][tile]
        weighted = (weight * matched[0][tile]).astype(jnp.bfloat16)
        weight = weight.astype(jnp.bfloat16)
        for block in range(2):
            slot = slot_ref[(step * tiles + tile) * 2 + block]
            lanes = slice(block * BS, (block + 1) * BS)
            out[slot, 0] = weighted[:, lanes]
            out[slot, 1] = weight[:, lanes]


def filtered(first, last, slots, slot, taps, exposure, variance, mask, halo):
    rows, columns = mask.shape
    height = last - first
    per_step = FILTER_COLUMNS // BS
    end = columns // BS - 1
    smem = pl.BlockSpec(memory_space=pltpu.SMEM)
    vmem = pl.BlockSpec(memory_space=pltpu.VMEM)
    image_specs = [
        pl.BlockSpec((rows, BS), lambda i: (0, jnp.maximum(i * per_step - 1, 0))),
        pl.BlockSpec((rows, FILTER_COLUMNS), lambda i: (0, i)),
        pl.BlockSpec((rows, BS), lambda i: (0, jnp.minimum((i + 1) * per_step, end))),
    ]
    return pl.pallas_call(
        functools.partial(filter_kernel, first, last),
        grid=(columns // FILTER_COLUMNS,),
        out_shape=jax.ShapeDtypeStruct((slots, 2, height, BS), jnp.bfloat16),
        in_specs=[smem, vmem] + image_specs * 2 + [image_specs[1], vmem],
        out_specs=pl.BlockSpec((slots, 2, height, BS), lambda i: (0, 0, 0, 0)),
        scratch_shapes=[
            pltpu.VMEM((2, height + 2 * HALO, FILTER_COLUMNS + 2 * BS), jnp.bfloat16),
            pltpu.VMEM((2, 4 * BS, 2 * BS), jnp.bfloat16),
            pltpu.VMEM((2, height, height + 2 * HALO), jnp.bfloat16),
        ],
        compiler_params=pltpu.CompilerParams(vmem_limit_bytes=VMEM),
        cost_estimate=pl.CostEstimate(
            flops=2 * 10**9, bytes_accessed=16 * 2**20, transcendentals=0
        ),
        name="filter",
    )(slot, taps, *[exposure] * 3, *[variance] * 3, mask, halo)


def map_kernel(pairs, split, table_ref, first_ref, second_ref, column_ref, spread_ref, place_ref):
    lanes = lax.broadcasted_iota(jnp.int32, (BS, BS), 1)
    rows = lax.broadcasted_iota(jnp.int32, (BS, BS), 0)
    group = lanes // BAND
    target = rows + lanes % BAND - BAND // 2
    facts = table_ref[...]
    pick = lax.broadcasted_iota(jnp.int32, (facts.shape[1], BS), 0)
    own = lax.broadcasted_iota(jnp.int32, (facts.shape[1], BS), 1) // BAND
    for index in range(2):
        chosen = (pick == own + index * 2 * pairs).astype(jnp.bfloat16)
        spread_ref[index] = jnp.dot(facts, chosen, preferred_element_type=jnp.float32)
    centre = (BS - 1) / 2.0
    place_ref[0] = rows.astype(jnp.float32) - centre
    inside = (target >= 0) & (target < BS)
    place_ref[1] = jnp.where(inside, target.astype(jnp.float32) - centre, 1e3)

    def build(slot):
        stretch = spread_ref[0, pl.ds(slot, 1), :]
        offset = spread_ref[1, pl.ds(slot, 1), :]
        x = (1.0 + stretch) * place_ref[0] + offset - place_ref[1]
        square = x * x * (math.pi / 3.0) ** 2
        sinc = jnp.full_like(x, 1.0 / math.factorial(21))
        for term in range(9, -1, -1):
            sinc = sinc * square + (-1.0) ** term / math.factorial(2 * term + 1)
        power = sinc * sinc
        value = power * (1.0 - (4.0 / 3.0) * power * square)
        value = jnp.where(jnp.abs(x) < 3.0, value, 0.0)
        for pair in range(pairs):
            for direction in range(2):
                index = pair * 2 + direction
                one = jnp.where(group == index, value, 0.0)
                shift = (-BAND // 2 - BAND * index) % BS
                turned = pltpu.roll(one, shift, 1, stride=1, stride_axis=0).astype(jnp.bfloat16)
                if direction == 0:
                    first_ref[slot, pair] = turned[:split]
                    second_ref[slot, pair] = turned[split:]
                else:
                    column_ref[slot, pair] = turned.T

    @pl.loop(0, column_ref.shape[0] // 2)
    def _(batch):
        build(batch * 2)
        build(batch * 2 + 1)


def make_maps(table, earlier, pairs, part, parts):
    slots = table.shape[0]
    heights = (EDGE, BS - EDGE, BS)
    steps = slots // parts // MAP_SLOTS

    def kernel(table_ref, *refs):
        map_kernel(pairs, EDGE, table_ref, *refs[-5:])

    return pl.pallas_call(
        kernel,
        grid=(steps,),
        out_shape=[jax.ShapeDtypeStruct((slots, pairs, height, BS), jnp.bfloat16) for height in heights],
        in_specs=[pl.BlockSpec((MAP_SLOTS, table.shape[1]), lambda i: (part * steps + i, 0))]
        + [pl.BlockSpec(memory_space=pl.ANY)] * (3 if earlier else 0),
        out_specs=[
            pl.BlockSpec((MAP_SLOTS, pairs, height, BS), lambda i: (part * steps + i, 0, 0, 0))
            for height in heights
        ],
        scratch_shapes=[
            pltpu.VMEM((2, MAP_SLOTS, BS), jnp.float32),
            pltpu.VMEM((2, BS, BS), jnp.float32),
        ],
        input_output_aliases={1: 0, 2: 1, 3: 2} if earlier else {},
        compiler_params=pltpu.CompilerParams(vmem_limit_bytes=VMEM),
        cost_estimate=pl.CostEstimate(
            flops=10**10, bytes_accessed=24 * 2**20, transcendentals=0
        ),
        name="maps",
    )(table, *(earlier or []))


def warp_kernel(count, aim_ref, *refs):
    blocks, row_ref, column_ref = refs[:count], refs[count], refs[count + 1]
    outs, total = refs[count + 2 : -1], refs[-1]
    step = pl.program_id(0)
    per_step, pairs, height, _ = row_ref.shape

    @pl.when(step == 0)
    def _():
        total[...] = jnp.zeros_like(total)

    for slot in range(per_step):
        source = jnp.concatenate(
            [jnp.concatenate([ref[slot, plane] for ref in blocks], axis=0) for plane in range(2)],
            axis=1,
        )
        stack = row_ref[slot].reshape(pairs * height, BS)[:, : source.shape[0]]
        half_warp = jnp.dot(stack, source, preferred_element_type=jnp.float32).astype(jnp.bfloat16)
        for pair in range(pairs):
            mine = half_warp[pair * height : (pair + 1) * height]
            both = jnp.concatenate([mine[:, :BS], mine[:, BS:]], axis=0)
            aim = aim_ref[(step * per_step + slot) * pairs + pair]
            total[aim] += jnp.dot(both, column_ref[slot, pair], preferred_element_type=jnp.float32)

    @pl.when(step == pl.num_programs(0) - 1)
    def _():
        for index, out in enumerate(outs):
            out[...] = total[index * PB_DEV : (index + 1) * PB_DEV].astype(out.dtype)


def warp(aims, blocks, row_maps, column_maps, groups):
    slots, pairs, height, _ = row_maps.shape

    def whole(array):
        return pl.BlockSpec((WARP_SLOTS,) + array.shape[1:], lambda i, _: (i, 0, 0, 0))

    operands = [*blocks, row_maps, column_maps]
    return pl.pallas_call(
        functools.partial(warp_kernel, len(blocks)),
        grid_spec=pltpu.PrefetchScalarGridSpec(
            num_scalar_prefetch=1,
            grid=(slots // WARP_SLOTS,),
            in_specs=[whole(array) for array in operands],
            out_specs=[pl.BlockSpec((PB_DEV, 2 * height, BS), lambda i, _: (0, 0, 0))] * groups,
            scratch_shapes=[pltpu.VMEM((groups * PB_DEV + 1, 2 * height, BS), jnp.float32)],
        ),
        out_shape=[
            jax.ShapeDtypeStruct(
                (PB_DEV, 2 * height, BS), jnp.float32 if index == 0 else jnp.bfloat16
            )
            for index in range(groups)
        ],
        compiler_params=pltpu.CompilerParams(vmem_limit_bytes=VMEM),
        cost_estimate=pl.CostEstimate(
            flops=6 * 10**9, bytes_accessed=32 * 2**20, transcendentals=0
        ),
        name="warp",
    )(aims, *operands)


def local(
    exposure, variance, pixel_mask, psf_kernel, block_owner, patch_index, pair_stretch, pair_offset
):
    _, rows, columns = exposure.shape
    block_count = columns // BS
    owners = lax.axis_size("sky")
    groups = lax.axis_size("visit")
    slots = owners * CAP
    pairs = patch_index.shape[-1]

    def exchange(array):
        return lax.all_to_all(array, "sky", split_axis=0, concat_axis=0, tiled=True)

    low = jnp.concatenate([exposure[:, rows - HALO :], variance[:, rows - HALO :]], axis=0)
    high = jnp.concatenate([exposure[:, :HALO], variance[:, :HALO]], axis=0)
    low, high, block_owner, patch_index, pair_stretch, pair_offset = lax.optimization_barrier(
        (low, high, block_owner, patch_index, pair_stretch, pair_offset)
    )
    top = lax.ppermute(low, "sky", [(i, i + 1) for i in range(owners - 1)])
    bottom = lax.ppermute(high, "sky", [(i + 1, i) for i in range(owners - 1)])

    facts = jnp.concatenate(
        [
            pair_stretch.reshape(-1),
            pair_offset.reshape(-1),
            patch_index.reshape(-1).astype(jnp.bfloat16),
            block_owner.reshape(-1).astype(jnp.bfloat16),
        ]
    )
    known = exchange(jnp.broadcast_to(facts[None], (owners, facts.shape[0])))

    owner = block_owner.reshape(block_count)
    order = jnp.arange(block_count)
    earlier = (owner[:, None] == owner[None, :]) & (order[None, :] < order[:, None])
    slot = owner * CAP + jnp.sum(earlier, axis=1).astype(jnp.int32)

    images = [array.reshape(rows, columns) for array in (exposure, variance, pixel_mask)]
    upper_planes = filtered(0, CUT, slots, slot, psf_kernel, *images, top)
    upper_planes, known, slot, bottom = lax.optimization_barrier(
        (upper_planes, known, slot, bottom)
    )
    first = exchange(upper_planes)

    lower_planes = filtered(CUT, rows, slots, slot, psf_kernel, *images, bottom)
    sizes = [2 * pairs * block_count, 2 * pairs * block_count, pairs * block_count, block_count]
    ends = [sum(sizes[: index + 1]) for index in range(len(sizes))]
    stretch, offset, patch, holder = (
        known[:, end - size : end].reshape(owners, block_count, -1).astype(jnp.float32)
        for end, size in zip(ends, sizes)
    )
    mine = holder[:, :, 0] == lax.axis_index("sky").astype(jnp.float32)
    rank = jnp.cumsum(mine.astype(jnp.int32), axis=1) - 1
    chosen = mine[:, None, :] & (rank[:, None, :] == jnp.arange(CAP)[None, :, None])
    chosen = chosen.astype(jnp.bfloat16)

    def picked(values):
        return jnp.einsum(
            "srb,sbf->srf",
            chosen,
            values.astype(jnp.bfloat16),
            preferred_element_type=jnp.float32,
        ).reshape(slots, -1)

    table = picked(jnp.concatenate([stretch, offset, patch, jnp.ones_like(holder)], axis=2))

    patch = table[:, 4 * pairs : 5 * pairs].astype(jnp.int32)
    distance = (patch // PB_DEV - lax.axis_index("visit")) % groups
    aims = jnp.where(
        table[:, 5 * pairs :] > 0.5, distance * PB_DEV + patch % PB_DEV, groups * PB_DEV
    )
    aims = aims.reshape(slots * pairs)
    maps = make_maps(table.astype(jnp.bfloat16), None, pairs, 0, 1)

    first, lower_planes, aims, *maps = lax.optimization_barrier((first, lower_planes, aims, *maps))
    first_maps, second_maps, column_maps = maps
    second = exchange(lower_planes)

    def coadd(sums):
        whole = sums[0]
        for step in range(1, groups):
            ring = [(i, (i + step) % groups) for i in range(groups)]
            whole = whole + lax.ppermute(sums[step], "visit", ring).astype(jnp.float32)
        height = whole.shape[1] // 2
        return whole[:, :height] / jnp.maximum(whole[:, height:], 1.0)

    upper = warp(aims, [first], first_maps, column_maps, groups)
    *upper, first = lax.optimization_barrier((*upper, first))
    lower = warp(aims, [first, second], second_maps, column_maps, groups)
    return jnp.concatenate([coadd(upper), coadd(lower)], axis=1)


def solution(mesh):
    return jax.shard_map(
        local,
        mesh=mesh,
        in_specs=(
            P("visit", "sky", None),
            P("visit", "sky", None),
            P("visit", "sky", None),
            P("visit", None, None),
            P("visit", "sky", None),
            P("visit", "sky", None, None),
            P("visit", "sky", None, None, None),
            P("visit", "sky", None, None, None),
        ),
        out_specs=P(("visit", "sky"), None, None),
        check_vma=False,
    )
```

```python
import functools
import math

import jax
import jax.numpy as jnp
from jax import lax
from jax.experimental import pallas as pl
from jax.experimental.pallas import tpu as pltpu
from jax.sharding import PartitionSpec as P

BS = 128
HALO = 16
BAND = 16
CAP = 2
PB_DEV = 8
CUT = 80
EDGE = CUT - 16
FACTS = 16
FILTER_COLUMNS = 1024
WARP_SLOTS = 16
FILTER_VMEM = 32 * 1024 * 1024
WARP_VMEM = 60 * 1024 * 1024


def toeplitz(rows, columns, shift, tap):
    lag = lax.broadcasted_iota(jnp.int32, (rows, columns), 0) - lax.broadcasted_iota(jnp.int32, (rows, columns), 1) + shift
    matrix = jnp.zeros((rows, columns), jnp.float32)
    for index, value in enumerate(tap):
        matrix = jnp.where(lag == index, value, matrix)
    return matrix.astype(jnp.bfloat16)

def filter_kernel(first, last, slot_ref, taps_ref, *refs):
    images, mask_ref, halo_ref = (refs[0:3], refs[3:6]), refs[6], refs[7]
    facts_ref, (out, framed, across_ref, down_ref) = refs[8:-4], refs[-4:]
    rows, columns = mask_ref.shape
    height = last - first
    tall = height + 2 * HALO
    wide = 2 * BS
    half = (taps_ref.shape[-1] - 1) // 2
    step, steps = pl.program_id(0), pl.num_programs(0)

    @pl.when(step == 0)
    def _():
        empty = jnp.zeros((BS, BS), jnp.bfloat16)
        values = taps_ref[0].astype(jnp.float32)
        for plane in range(2):
            taps = [
                [values[way : way + 1, tap : tap + 1] for tap in range(taps_ref.shape[-1])]
                for way in range(2)
            ]
            if plane == 1:
                taps = [[tap * tap for tap in way] for way in taps]
            left, middle, right = (toeplitz(BS, BS, half + by * BS, taps[0]) for by in (-1, 0, 1))
            pattern = ((left, empty), (middle, left), (right, middle), (empty, right))
            for row, blocks in enumerate(pattern):
                across_ref[plane, row * BS : (row + 1) * BS, :BS] = blocks[0]
                across_ref[plane, row * BS : (row + 1) * BS, BS:] = blocks[1]
            down_ref[plane] = toeplitz(height, tall, half + HALO, taps[1][::-1])

        for ref in facts_ref:
            out[:, 2 * height :, :] = jnp.zeros((out.shape[0], FACTS, BS), jnp.bfloat16)

    start = pl.multiple_of(step * columns, columns)
    before = pl.multiple_of(jnp.maximum(start - BS, 0), BS)
    after = pl.multiple_of(jnp.minimum(start + columns, (steps - 1) * columns - BS + columns), BS)
    for plane, parts in enumerate(images):
        halo = [
            halo_ref[plane, :, pl.ds(before, BS)],
            halo_ref[plane, :, pl.ds(start, columns)],
            halo_ref[plane, :, pl.ds(after, BS)],
        ]
        if first == 0:
            strips = ((0, halo), (HALO, [part[: last + HALO, :] for part in parts]))
        else:
            strips = (
                (0, [part[first - HALO :, :] for part in parts]),
                (rows - first + HALO, halo),
            )
        for row, pieces in strips:
            column = 0
            for piece, kept in zip(pieces, (step > 0, None, step < steps - 1)):
                if kept is not None:
                    piece = jnp.where(kept, piece, jnp.zeros_like(piece))
                framed[
                    plane, row : row + piece.shape[0], column : column + piece.shape[1]
                ] = piece
                column += piece.shape[1]

    tiles = columns // wide
    matched = []
    for plane in range(2):
        stack = jnp.concatenate(
            [framed[plane, :, tile * wide : tile * wide + 4 * BS] for tile in range(tiles)], axis=0
        )
        passed = jnp.dot(stack, across_ref[plane], preferred_element_type=jnp.float32).astype(
            jnp.bfloat16
        )
        matched.append(
            [
                jnp.dot(
                    down_ref[plane],
                    passed[tile * tall : (tile + 1) * tall],
                    preferred_element_type=jnp.float32,
                )
                for tile in range(tiles)
            ]
        )
    for tile in range(tiles):
        usable = mask_ref[first:last, tile * wide : (tile + 1) * wide].astype(jnp.float32)
        weight = usable / matched[1][tile]
        weighted = (weight * matched[0][tile]).astype(jnp.bfloat16)
        weight = weight.astype(jnp.bfloat16)
        for block in range(2):
            index = (step * tiles + tile) * 2 + block
            slot = slot_ref[index]
            lanes = slice(block * BS, (block + 1) * BS)
            out[slot, :height, :] = weighted[:, lanes]
            out[slot, height : 2 * height, :] = weight[:, lanes]
            for ref in facts_ref:
                row = jnp.broadcast_to(ref[pl.ds(index, 1), :], (FACTS, BS))
                out[slot, 2 * height :, :] = row.astype(jnp.bfloat16)


def filtered(first, last, slots, slot, taps, exposure, variance, mask, halo, *facts):
    rows, columns = mask.shape
    height = last - first
    tall = 2 * height + (FACTS if facts else 0)
    per_step = FILTER_COLUMNS // BS
    end = columns // BS - 1
    smem = pl.BlockSpec(memory_space=pltpu.SMEM)
    vmem = pl.BlockSpec(memory_space=pltpu.VMEM)
    image_specs = [
        pl.BlockSpec((rows, BS), lambda i: (0, jnp.maximum(i * per_step - 1, 0))),
        pl.BlockSpec((rows, FILTER_COLUMNS), lambda i: (0, i)),
        pl.BlockSpec((rows, BS), lambda i: (0, jnp.minimum((i + 1) * per_step, end))),
    ]
    return pl.pallas_call(
        functools.partial(filter_kernel, first, last),
        grid=(columns // FILTER_COLUMNS,),
        out_shape=jax.ShapeDtypeStruct((slots, tall, BS), jnp.bfloat16),
        in_specs=[smem, vmem] + image_specs * 2 + [image_specs[1], vmem] + [vmem] * len(facts),
        out_specs=pl.BlockSpec((slots, tall, BS), lambda i: (0, 0, 0)),
        scratch_shapes=[
            pltpu.VMEM((2, height + 2 * HALO, FILTER_COLUMNS + 2 * BS), jnp.bfloat16),
            pltpu.VMEM((2, 4 * BS, 2 * BS), jnp.bfloat16),
            pltpu.VMEM((2, height, height + 2 * HALO), jnp.bfloat16),
        ],
        compiler_params=pltpu.CompilerParams(vmem_limit_bytes=FILTER_VMEM),
        cost_estimate=pl.CostEstimate(
            flops=2 * 10**9, bytes_accessed=16 * 2**20, transcendentals=0
        ),
        name="filter",
    )(slot, taps, *[exposure] * 3, *[variance] * 3, mask, halo, *facts)


def series(square, count, odd):
    total = jnp.zeros_like(square)
    for term in range(count, -1, -1):
        total = total * square + (-1.0) ** term / math.factorial(2 * term + odd)
    return total


def accumulate(total, aims, rows, source, columns):
    height = rows.shape[0] // len(columns)
    half_warp = jnp.dot(rows, source, preferred_element_type=jnp.float32).astype(jnp.bfloat16)
    for pair, column in enumerate(columns):
        mine = half_warp[pair * height : (pair + 1) * height]
        both = jnp.concatenate([mine[:, :BS], mine[:, BS:]], axis=0)
        total[aims[pair]] += jnp.dot(both, column, preferred_element_type=jnp.float32)


def upper_kernel(
    pairs, unroll, aim_ref, table_ref, block_ref, second_ref, column_ref, *refs
):
    outs, (total, spread_ref, place_ref, near_ref, taps_ref) = refs[:-5], refs[-5:]
    step = pl.program_id(0)
    per_step = column_ref.shape[0]
    half = per_step // 2
    lanes = lax.broadcasted_iota(jnp.int32, (BS, BS), 1)
    rows = lax.broadcasted_iota(jnp.int32, (BS, BS), 0)
    group = lanes // BAND
    centre = (BS - 1) / 2.0

    @pl.when(step == 0)
    def _():
        total[...] = jnp.zeros_like(total)
        target = rows + lanes % BAND - BAND // 2
        inside = (target >= 0) & (target < BS)
        place_ref[0] = rows.astype(jnp.float32) - centre
        place_ref[1] = jnp.where(inside, target.astype(jnp.float32) - centre, 1e3)

    facts = table_ref[...]
    low, high = facts[:half].astype(jnp.bfloat16), facts[half:].astype(jnp.bfloat16)
    facts = facts.astype(jnp.bfloat16)

    def sent(values, chosen):
        return jnp.dot(values, chosen.astype(jnp.bfloat16), preferred_element_type=jnp.float32)

    for kind in range(2):
        field = 2 * pairs * kind
        spread_ref[kind] = sent(low, (rows == field + 2 * group) & (group < pairs)) + sent(
            high, (rows == field + 2 * (group - pairs)) & (group >= pairs)
        )
    pixels = lanes[:per_step].astype(jnp.float32) - centre
    for pair in range(pairs):
        stretch = sent(facts, rows == 2 * pair + 1)
        offset = sent(facts, rows == 2 * pairs + 2 * pair + 1)
        source = (1.0 + stretch) * pixels + centre + offset
        near = jnp.round(source)
        x = source - near
        near_ref[pair] = near
        whole, third = math.pi * x, (math.pi / 3.0) * x
        whole_sinc = series(whole * whole, 8, 1)
        third_sinc = series(third * third, 8, 1)
        third_cos = series(third * third, 8, 0)
        for k in range(-3, 4):
            if k == 0:
                value = whole_sinc * third_sinc
            else:
                angle = math.pi * k / 3.0
                slow = third_sinc * third * math.cos(angle) - third_cos * math.sin(angle)
                far = x - k
                value = ((-1.0) ** k * 3.0 / math.pi**2) * whole_sinc * whole * slow / (far * far)
                value = jnp.where(jnp.abs(far) < 3.0, value, 0.0)
            taps_ref[k + 3, pair] = value

    numbers = rows.astype(jnp.bfloat16)

    def build(m):
        stretch = spread_ref[0, pl.ds(m, 1), :]
        offset = spread_ref[1, pl.ds(m, 1), :]
        x = (1.0 + stretch) * place_ref[0] + offset - place_ref[1]
        square = x * x * (math.pi / 3.0) ** 2
        power = series(square, 10, 1)
        power = power * power
        value = power * (1.0 - (4.0 / 3.0) * power * square)
        value = jnp.where(jnp.abs(x) < 3.0, value, 0.0)
        for part in range(2):
            slot = m + part * half
            stack, columns = [], []
            for pair in range(pairs):
                index = part * pairs + pair
                one = jnp.where(group == index, value, 0.0)
                shift = (-BAND // 2 - BAND * index) % BS
                turned = pltpu.roll(one, shift, 1, stride=1, stride_axis=0).astype(jnp.bfloat16)
                second_ref[slot, pair] = turned[EDGE:]
                stack.append(turned[:EDGE, :CUT])
                lag = numbers - near_ref[pair, pl.ds(slot, 1), :].astype(jnp.bfloat16)
                column = jnp.zeros((BS, BS), jnp.bfloat16)
                for k in range(7):
                    tap = taps_ref[k, pair, pl.ds(slot, 1), :].astype(jnp.bfloat16)
                    column = jnp.where(lag == jnp.bfloat16(k - 3), tap, column)
                column_ref[slot, pair] = column
                columns.append(column)
            source = jnp.concatenate(
                [block_ref[slot, :CUT, :], block_ref[slot, CUT : 2 * CUT, :]], axis=1
            )
            aims = [aim_ref[(step * per_step + slot) * pairs + pair] for pair in range(pairs)]
            accumulate(total, aims, jnp.concatenate(stack, axis=0), source, columns)

    @pl.loop(0, half // unroll)
    def _(batch):
        for inner in range(unroll):
            build(batch * unroll + inner)

    @pl.when(step == pl.num_programs(0) - 1)
    def _():
        for index, out in enumerate(outs):
            out[...] = total[index * PB_DEV : (index + 1) * PB_DEV].astype(out.dtype)


def upper_warp(aims, table, first, pairs, groups, unroll=2):
    slots = first.shape[0]
    return pl.pallas_call(
        functools.partial(upper_kernel, pairs, unroll),
        grid_spec=pltpu.PrefetchScalarGridSpec(
            num_scalar_prefetch=1,
            grid=(slots // WARP_SLOTS,),
            in_specs=[
                pl.BlockSpec((WARP_SLOTS, BS), lambda i, _: (i, 0)),
                pl.BlockSpec((WARP_SLOTS,) + first.shape[1:], lambda i, _: (i, 0, 0)),
            ],
            out_specs=[
                pl.BlockSpec((WARP_SLOTS, pairs, BS - EDGE, BS), lambda i, _: (i, 0, 0, 0)),
                pl.BlockSpec((WARP_SLOTS, pairs, BS, BS), lambda i, _: (i, 0, 0, 0)),
            ]
            + [pl.BlockSpec((PB_DEV, 2 * EDGE, BS), lambda i, _: (0, 0, 0))] * groups,
            scratch_shapes=[
                pltpu.VMEM((groups * PB_DEV + 1, 2 * EDGE, BS), jnp.float32),
                pltpu.VMEM((2, WARP_SLOTS // 2, BS), jnp.float32),
                pltpu.VMEM((2, BS, BS), jnp.float32),
                pltpu.VMEM((pairs, WARP_SLOTS, BS), jnp.float32),
                pltpu.VMEM((7, pairs, WARP_SLOTS, BS), jnp.float32),
            ],
        ),
        out_shape=[
            jax.ShapeDtypeStruct((slots, pairs, BS - EDGE, BS), jnp.bfloat16),
            jax.ShapeDtypeStruct((slots, pairs, BS, BS), jnp.bfloat16),
        ]
        + [
            jax.ShapeDtypeStruct(
                (PB_DEV, 2 * EDGE, BS), jnp.float32 if index == 0 else jnp.bfloat16
            )
            for index in range(groups)
        ],
        compiler_params=pltpu.CompilerParams(vmem_limit_bytes=WARP_VMEM),
        cost_estimate=pl.CostEstimate(
            flops=10**10, bytes_accessed=32 * 2**20, transcendentals=0
        ),
        name="upper_warp",
    )(aims, table, first)


def lower_kernel(pairs, aim_ref, first_ref, second_ref, row_ref, column_ref, *refs):
    outs, total = refs[:-1], refs[-1]
    step = pl.program_id(0)
    per_step = column_ref.shape[0]

    @pl.when(step == 0)
    def _():
        total[...] = jnp.zeros_like(total)

    for slot in range(per_step):
        source = jnp.concatenate(
            [
                jnp.concatenate(
                    [
                        first_ref[slot, plane * CUT : (plane + 1) * CUT, :],
                        second_ref[slot, plane * (BS - CUT) : (plane + 1) * (BS - CUT), :],
                    ],
                    axis=0,
                )
                for plane in range(2)
            ],
            axis=1,
        )
        aims = [aim_ref[(step * per_step + slot) * pairs + pair] for pair in range(pairs)]
        rows = row_ref[slot].reshape(pairs * row_ref.shape[2], BS)
        columns = [column_ref[slot, pair] for pair in range(pairs)]
        accumulate(total, aims, rows, source, columns)

    @pl.when(step == pl.num_programs(0) - 1)
    def _():
        for index, out in enumerate(outs):
            out[...] = total[index * PB_DEV : (index + 1) * PB_DEV].astype(out.dtype)


def lower_warp(aims, first, second, row_maps, column_maps, groups):
    slots, pairs, height, _ = row_maps.shape

    def whole(array):
        return pl.BlockSpec(
            (WARP_SLOTS,) + array.shape[1:], lambda i, _: (i,) + (0,) * (array.ndim - 1)
        )

    operands = [first, second, row_maps, column_maps]
    return pl.pallas_call(
        functools.partial(lower_kernel, pairs),
        grid_spec=pltpu.PrefetchScalarGridSpec(
            num_scalar_prefetch=1,
            grid=(slots // WARP_SLOTS,),
            in_specs=[whole(array) for array in operands],
            out_specs=[pl.BlockSpec((PB_DEV, 2 * height, BS), lambda i, _: (0, 0, 0))] * groups,
            scratch_shapes=[pltpu.VMEM((groups * PB_DEV + 1, 2 * height, BS), jnp.float32)],
        ),
        out_shape=[
            jax.ShapeDtypeStruct(
                (PB_DEV, 2 * height, BS), jnp.float32 if index == 0 else jnp.bfloat16
            )
            for index in range(groups)
        ],
        compiler_params=pltpu.CompilerParams(vmem_limit_bytes=WARP_VMEM),
        cost_estimate=pl.CostEstimate(
            flops=6 * 10**9, bytes_accessed=32 * 2**20, transcendentals=0
        ),
        name="lower_warp",
    )(aims, *operands)


def local(
    exposure, variance, pixel_mask, psf_kernel, block_owner, patch_index, pair_stretch, pair_offset
):
    _, rows, columns = exposure.shape
    block_count = columns // BS
    owners = lax.axis_size("sky")
    groups = lax.axis_size("visit")
    slots = owners * CAP
    pairs = patch_index.shape[-1]

    def exchange(array):
        return lax.all_to_all(array, "sky", split_axis=0, concat_axis=0, tiled=True)

    low = jnp.concatenate([exposure[:, rows - HALO :], variance[:, rows - HALO :]], axis=0)
    high = jnp.concatenate([exposure[:, :HALO], variance[:, :HALO]], axis=0)
    top = lax.ppermute(low, "sky", [(i, i + 1) for i in range(owners - 1)])
    bottom = lax.ppermute(high, "sky", [(i + 1, i) for i in range(owners - 1)])

    owner = block_owner.reshape(block_count)
    order = jnp.arange(block_count)
    earlier = (owner[:, None] == owner[None, :]) & (order[None, :] < order[:, None])
    slot = owner * CAP + jnp.sum(earlier, axis=1).astype(jnp.int32)
    facts = jnp.concatenate(
        [
            pair_stretch.reshape(block_count, 2 * pairs).astype(jnp.float32),
            pair_offset.reshape(block_count, 2 * pairs).astype(jnp.float32),
            patch_index.reshape(block_count, pairs).astype(jnp.float32),
            jnp.ones((block_count, BS - 5 * pairs), jnp.float32),
        ],
        axis=1,
    )

    images = [array.reshape(rows, columns) for array in (exposure, variance, pixel_mask)]
    upper_planes = filtered(0, CUT, slots, slot, psf_kernel, *images, top, facts)
    upper_planes, slot, bottom = lax.optimization_barrier((upper_planes, slot, bottom))
    first = exchange(upper_planes)

    lower_planes = filtered(CUT, rows, slots, slot, psf_kernel, *images, bottom)
    first, lower_planes = lax.optimization_barrier((first, lower_planes))
    second = exchange(lower_planes)

    table = first[:, 2 * CUT, :].astype(jnp.float32)
    patch = table[:, 4 * pairs : 5 * pairs].astype(jnp.int32)
    distance = (patch // PB_DEV - lax.axis_index("visit")) % groups
    aims = jnp.where(
        table[:, 5 * pairs : 5 * pairs + 1] > 0.5,
        distance * PB_DEV + patch % PB_DEV,
        groups * PB_DEV,
    )
    aims = aims.reshape(slots * pairs)
    second_maps, column_maps, *upper = upper_warp(aims, table, first, pairs, groups)

    def coadd(sums):
        whole = sums[0]
        for step in range(1, groups):
            ring = [(i, (i + step) % groups) for i in range(groups)]
            whole = whole + lax.ppermute(sums[step], "visit", ring).astype(jnp.float32)
        height = whole.shape[1] // 2
        return whole[:, :height] / jnp.maximum(whole[:, height:], 1.0)

    lower = lower_warp(aims, first, second, second_maps, column_maps, groups)
    return jnp.concatenate([coadd(upper), coadd(lower)], axis=1)


def solution(mesh):
    return jax.shard_map(
        local,
        mesh=mesh,
        in_specs=(
            P("visit", "sky", None),
            P("visit", "sky", None),
            P("visit", "sky", None),
            P("visit", None, None),
            P("visit", "sky", None),
            P("visit", "sky", None, None),
            P("visit", "sky", None, None, None),
            P("visit", "sky", None, None, None),
        ),
        out_specs=P(("visit", "sky"), None, None),
        check_vma=False,
    )
```

```python
import functools
import math

import jax
import jax.numpy as jnp
from jax import lax
from jax.experimental import pallas as pl
from jax.experimental.pallas import tpu as pltpu
from jax.sharding import PartitionSpec as P

BS = 128
HALO = 16
BAND = 16
CAP = 2
PB_DEV = 8
CUT = 80
EDGE = CUT - 16
REACH = EDGE - 16
FACTS = 16
FILTER_COLUMNS = 2048
UNROLL = 2
UPPER_PARTS = 4
FILTER_VMEM = 60 * 1024 * 1024
UPPER_VMEM = 60 * 1024 * 1024
LOWER_VMEM = 58 * 1024 * 1024
LOWER_PARTS = 4


def toeplitz(rows, columns, shift, tap):
    lag = lax.broadcasted_iota(jnp.int32, (rows, columns), 0) - lax.broadcasted_iota(jnp.int32, (rows, columns), 1) + shift
    matrix = jnp.zeros((rows, columns), jnp.float32)
    for index, value in enumerate(tap):
        matrix = jnp.where(lag == index, value, matrix)
    return matrix.astype(jnp.bfloat16)

def filter_kernel(span, chunk, side, owners, owner_ref, taps_ref, *refs):
    exposure_ref, variance_ref, mask_ref, halo_ref = refs[:4]
    pair_refs, out = refs[4:-14], refs[-14]
    framed, usable_ref, across_ref, down_ref, staged, empty_ref, facts_ref = refs[-13:-6]
    slot_ref, count_ref, here, near, done, cleared = refs[-6:]
    (first, last), (chunk_first, chunk_last) = span, chunk
    rows, columns = mask_ref.shape
    height, chunk_height = last - first, chunk_last - chunk_first
    tall = height + 2 * HALO
    wide = 2 * BS
    half = (taps_ref.shape[-1] - 1) // 2
    parts = here.shape[1]
    part_columns = columns // parts

    own_from, own_to = max(first - HALO, 0), min(last + HALO, rows)
    own_at, halo_at = (HALO, 0) if side == "top" else (0, own_to - own_from)

    def fetched(part):
        lanes = pl.ds(part * part_columns, part_columns)
        inner = pl.ds(BS + part * part_columns, part_columns)
        own, placed = pl.ds(own_from, own_to - own_from), pl.ds(own_at, own_to - own_from)
        kept = pl.ds(first, height)
        return [
            pltpu.make_async_copy(
                exposure_ref.at[own, lanes], framed.at[0, placed, inner], here.at[0, part]
            ),
            pltpu.make_async_copy(
                variance_ref.at[own, lanes], framed.at[1, placed, inner], here.at[1, part]
            ),
            pltpu.make_async_copy(
                mask_ref.at[kept, lanes], usable_ref.at[:, lanes], here.at[2, part]
            ),
        ]

    halos = [
        pltpu.make_async_copy(
            halo_ref.at[plane],
            framed.at[plane, pl.ds(halo_at, HALO), pl.ds(BS, columns)],
            near.at[plane],
        )
        for plane in range(2)
    ]
    for copy in halos:
        copy.start()
    for part in range(parts):
        for copy in fetched(part):
            copy.start()
    if pair_refs:
        empty_ref[...] = jnp.zeros(empty_ref.shape, jnp.bfloat16)
        clear = pltpu.make_async_copy(
            empty_ref, out.at[:, pl.ds(2 * chunk_height, FACTS), :], cleared.at[0]
        )
        clear.start()

    for owner in range(count_ref.shape[0]):
        count_ref[owner] = 0
    for block in range(slot_ref.shape[0]):
        owner = owner_ref[0, 0, block]
        rank = count_ref[owner]
        slot_ref[block] = owner * CAP + rank
        count_ref[owner] = rank + 1

    if pair_refs:
        stretch_ref, offset_ref, patch_ref = pair_refs
        pairs, blocks = patch_ref.shape
        facts_ref[...] = jnp.ones(facts_ref.shape, jnp.float32)
        for pair in range(pairs):
            for base, ref in ((0, stretch_ref), (2 * pairs, offset_ref)):
                facts_ref[base + 2 * pair : base + 2 * pair + 2, :blocks] = ref[pair].astype(
                    jnp.float32
                )
        facts_ref[4 * pairs : 5 * pairs, :blocks] = patch_ref[...].astype(jnp.float32)
        facts_ref[...] = facts_ref[...].T

    margin = jnp.zeros((tall, BS), jnp.bfloat16)
    empty = jnp.zeros((BS, BS), jnp.bfloat16)
    values = taps_ref[0].astype(jnp.float32)
    for plane in range(2):
        framed[plane, :, :BS] = margin
        framed[plane, :, BS + columns :] = margin
        taps = [
            [values[way : way + 1, tap : tap + 1] for tap in range(taps_ref.shape[-1])]
            for way in range(2)
        ]
        if plane == 1:
            taps = [[tap * tap for tap in way] for way in taps]
        left, middle, right = (toeplitz(BS, BS, half + by * BS, taps[0]) for by in (-1, 0, 1))
        pattern = ((left, empty), (middle, left), (right, middle), (empty, right))
        for row, blocks in enumerate(pattern):
            across_ref[plane, row * BS : (row + 1) * BS, :BS] = blocks[0]
            across_ref[plane, row * BS : (row + 1) * BS, BS:] = blocks[1]
        down_ref[plane] = toeplitz(height, tall, half + HALO, taps[1][::-1])

    for copy in halos:
        copy.wait()
    outermost = 0 if side == "top" else owners - 1
    inner = lax.axis_index("sky") != outermost
    for plane in range(2):
        halo = framed[plane, halo_at : halo_at + HALO, :]
        framed[plane, halo_at : halo_at + HALO, :] = jnp.where(inner, halo, jnp.zeros_like(halo))
    for copy in fetched(0):
        copy.wait()
    tiles = part_columns // wide
    sent = []
    for part in range(parts):
        if part + 1 < parts:
            for copy in fetched(part + 1):
                copy.wait()
        base = part * part_columns
        matched = []
        for plane in range(2):
            stack = jnp.concatenate(
                [
                    framed[plane, :, base + tile * wide : base + tile * wide + 4 * BS]
                    for tile in range(tiles)
                ],
                axis=0,
            )
            passed = jnp.dot(
                stack, across_ref[plane], preferred_element_type=jnp.float32
            ).astype(jnp.bfloat16)
            matched.append(
                [
                    jnp.dot(
                        down_ref[plane],
                        passed[tile * tall : (tile + 1) * tall],
                        preferred_element_type=jnp.float32,
                    )
                    for tile in range(tiles)
                ]
            )
        for tile in range(tiles):
            lanes = slice(base + tile * wide, base + (tile + 1) * wide)
            weight = usable_ref[:, lanes].astype(jnp.float32) / matched[1][tile]
            weighted = (weight * matched[0][tile]).astype(jnp.bfloat16)
            weight = weight.astype(jnp.bfloat16)
            for block in range(2):
                index = (part * tiles + tile) * 2 + block
                lanes = slice(block * BS, (block + 1) * BS)
                staged[index, :height, :] = weighted[:, lanes]
                staged[index, height : 2 * height, :] = weight[:, lanes]
                if pair_refs:
                    row = jnp.broadcast_to(facts_ref[index : index + 1, :], (FACTS, BS))
                    staged[index, 2 * height :, :] = row.astype(jnp.bfloat16)
        if pair_refs and part == 0:
            clear.wait()
        at = first - chunk_first
        pieces = [(0, height, at), (height, height, chunk_height + at)]
        if pair_refs:
            pieces[1] = (height, height + FACTS, chunk_height + at)
        for index in range(part * tiles * 2, (part + 1) * tiles * 2):
            for piece, (begin, count, to) in enumerate(pieces):
                copy = pltpu.make_async_copy(
                    staged.at[index, pl.ds(begin, count), :],
                    out.at[slot_ref[index], pl.ds(to, count), :],
                    done.at[index, piece],
                )
                copy.start()
                sent.append(copy)
    for copy in sent:
        copy.wait()


def filtered(span, chunk, owners, owner, taps, images, side, halo, facts=()):
    rows, columns = images[2].shape
    height = span[1] - span[0]
    tall = 2 * (chunk[1] - chunk[0]) + (0 if chunk[0] else FACTS)
    slots = owners * CAP
    blocks = columns // BS
    parts = columns // FILTER_COLUMNS
    smem = pl.BlockSpec(memory_space=pltpu.SMEM)
    hbm = pl.BlockSpec(memory_space=pltpu.HBM)

    def whole(array):
        return pl.BlockSpec(array.shape, lambda i: (0,) * array.ndim)

    operands = [owner, taps, *images, halo, *facts]
    specs = [smem, whole(taps), hbm, hbm, hbm, pl.BlockSpec(memory_space=pl.ANY)]
    specs += [whole(fact) for fact in facts]
    return pl.pallas_call(
        functools.partial(filter_kernel, span, chunk, side, owners),
        grid=(1,),
        out_shape=jax.ShapeDtypeStruct((slots, tall, BS), jnp.bfloat16),
        in_specs=specs,
        out_specs=hbm,
        scratch_shapes=[
            pltpu.VMEM((2, height + 2 * HALO, columns + 2 * BS), jnp.bfloat16),
            pltpu.VMEM((height, columns), jnp.int32),
            pltpu.VMEM((2, 4 * BS, 2 * BS), jnp.bfloat16),
            pltpu.VMEM((2, height, height + 2 * HALO), jnp.bfloat16),
            pltpu.VMEM((blocks, 2 * height + FACTS, BS), jnp.bfloat16),
            pltpu.VMEM((slots, FACTS, BS), jnp.bfloat16),
            pltpu.VMEM((BS, BS), jnp.float32),
            pltpu.SMEM((blocks,), jnp.int32),
            pltpu.SMEM((owners,), jnp.int32),
            pltpu.SemaphoreType.DMA((3, parts)),
            pltpu.SemaphoreType.DMA((2,)),
            pltpu.SemaphoreType.DMA((blocks, 2)),
            pltpu.SemaphoreType.DMA((1,)),
        ],
        compiler_params=pltpu.CompilerParams(vmem_limit_bytes=FILTER_VMEM),
        cost_estimate=pl.CostEstimate(
            flops=2 * 10**9, bytes_accessed=16 * 2**20, transcendentals=0
        ),
        name="filter",
    )(*operands)


def series(square, count, odd):
    total = jnp.zeros_like(square)
    for term in range(count, -1, -1):
        total = total * square + (-1.0) ** term / math.factorial(2 * term + odd)
    return total


def accumulate(total, aims, rows, source, columns):
    height = rows.shape[0] // len(columns)
    half_warp = jnp.dot(rows, source, preferred_element_type=jnp.float32).astype(jnp.bfloat16)
    for pair, column in enumerate(columns):
        mine = half_warp[pair * height : (pair + 1) * height]
        both = jnp.concatenate([mine[:, :BS], mine[:, BS:]], axis=0)
        total[aims[pair]] += jnp.dot(both, column, preferred_element_type=jnp.float32)


def upper_kernel(pairs, aim_ref, table_ref, first_ref, second_out, column_out, *refs):
    outs, (block_ref, second_ref, column_ref, arrived, left) = refs[:-10], refs[-10:-5]
    total, spread_ref, place_ref, near_ref, taps_ref = refs[-5:]
    parts = arrived.shape[1]
    half = table_ref.shape[0] // 2
    per_part = half // parts
    lanes = lax.broadcasted_iota(jnp.int32, (BS, BS), 1)
    rows = lax.broadcasted_iota(jnp.int32, (BS, BS), 0)
    group = lanes // BAND
    centre = (BS - 1) / 2.0

    def fetched(part):
        return [
            pltpu.make_async_copy(
                first_ref.at[pl.ds(base + part * per_part, per_part), pl.ds(0, 2 * CUT), :],
                block_ref.at[pl.ds(base + part * per_part, per_part)],
                arrived.at[index, part],
            )
            for index, base in enumerate((0, half))
        ]

    def returned(part):
        return [
            pltpu.make_async_copy(
                kept.at[pl.ds(base + part * per_part, per_part)],
                out.at[pl.ds(base + part * per_part, per_part)],
                left.at[2 * kind + index, part],
            )
            for index, base in enumerate((0, half))
            for kind, (kept, out) in enumerate(((second_ref, second_out), (column_ref, column_out)))
        ]

    for part in range(parts):
        for copy in fetched(part):
            copy.start()
    total[...] = jnp.zeros_like(total)
    target = rows + lanes % BAND - BAND // 2
    inside = (target >= 0) & (target < BS)
    place_ref[0] = rows.astype(jnp.float32) - centre
    place_ref[1] = jnp.where(inside, target.astype(jnp.float32) - centre, 1e3)

    facts = table_ref[...].astype(jnp.bfloat16)

    def sent(values, chosen):
        return jnp.dot(values, chosen.astype(jnp.bfloat16), preferred_element_type=jnp.float32)

    for kind in range(2):
        field = 2 * pairs * kind
        spread_ref[kind] = sent(
            facts[:half], (rows == field + 2 * group) & (group < pairs)
        ) + sent(facts[half:], (rows == field + 2 * (group - pairs)) & (group >= pairs))
    pixels = lanes[: 2 * half].astype(jnp.float32) - centre
    for pair in range(pairs):
        stretch = sent(facts, rows == 2 * pair + 1)
        offset = sent(facts, rows == 2 * pairs + 2 * pair + 1)
        source = (1.0 + stretch) * pixels + centre + offset
        near = jnp.round(source)
        x = source - near
        near_ref[pair] = near
        whole, third = math.pi * x, (math.pi / 3.0) * x
        whole_sinc = series(whole * whole, 8, 1)
        third_sinc = series(third * third, 8, 1)
        third_cos = series(third * third, 8, 0)
        for k in range(-3, 4):
            if k == 0:
                value = whole_sinc * third_sinc
            else:
                angle = math.pi * k / 3.0
                slow = third_sinc * third * math.cos(angle) - third_cos * math.sin(angle)
                far = x - k
                value = ((-1.0) ** k * 3.0 / math.pi**2) * whole_sinc * whole * slow / (far * far)
                value = jnp.where(jnp.abs(far) < 3.0, value, 0.0)
            taps_ref[k + 3, pair] = value

    numbers = rows.astype(jnp.bfloat16)

    def build(m):
        stretch = spread_ref[0, pl.ds(m, 1), :]
        offset = spread_ref[1, pl.ds(m, 1), :]
        x = (1.0 + stretch) * place_ref[0] + offset - place_ref[1]
        square = x * x * (math.pi / 3.0) ** 2
        power = series(square, 10, 1)
        power = power * power
        value = power * (1.0 - (4.0 / 3.0) * power * square)
        value = jnp.where(jnp.abs(x) < 3.0, value, 0.0)
        for which in range(2):
            slot = m + which * half
            stack, columns = [], []
            for pair in range(pairs):
                index = which * pairs + pair
                one = jnp.where(group == index, value, 0.0)
                shift = -BAND // 2 - BAND * index
                upper = pltpu.roll(one[:EDGE], shift % BS, 1, stride=1, stride_axis=0)
                lower = pltpu.roll(
                    one[EDGE:], (shift + EDGE - REACH) % BS, 1, stride=1, stride_axis=0
                )
                second_ref[slot, pair] = lower.astype(jnp.bfloat16)
                stack.append(upper.astype(jnp.bfloat16)[:, :CUT])
                lag = numbers - near_ref[pair, pl.ds(slot, 1), :].astype(jnp.bfloat16)
                column = jnp.zeros((BS, BS), jnp.bfloat16)
                for k in range(7):
                    tap = taps_ref[k, pair, pl.ds(slot, 1), :].astype(jnp.bfloat16)
                    column = jnp.where(lag == jnp.bfloat16(k - 3), tap, column)
                column_ref[slot, pair] = column
                columns.append(column)
            source = jnp.concatenate(
                [block_ref[slot, :CUT, :], block_ref[slot, CUT : 2 * CUT, :]], axis=1
            )
            aims = [aim_ref[slot * pairs + pair] for pair in range(pairs)]
            accumulate(total, aims, jnp.concatenate(stack, axis=0), source, columns)

    @pl.loop(0, parts)
    def _(part):
        for copy in fetched(part):
            copy.wait()

        @pl.loop(0, per_part // UNROLL)
        def _(batch):
            for inner in range(UNROLL):
                build(part * per_part + batch * UNROLL + inner)

        for copy in returned(part):
            copy.start()

    for index, out in enumerate(outs):
        out[...] = total[index * PB_DEV : (index + 1) * PB_DEV].astype(out.dtype)
    for part in range(parts):
        for copy in returned(part):
            copy.wait()


def upper_warp(aims, table, first, pairs, groups):
    slots = first.shape[0]
    second = jax.ShapeDtypeStruct((slots, pairs, BS - EDGE, BS), jnp.bfloat16)
    column = jax.ShapeDtypeStruct((slots, pairs, BS, BS), jnp.bfloat16)
    hbm = pl.BlockSpec(memory_space=pltpu.HBM)
    return pl.pallas_call(
        functools.partial(upper_kernel, pairs),
        grid=(1,),
        in_specs=[
            pl.BlockSpec(memory_space=pltpu.SMEM),
            pl.BlockSpec(table.shape, lambda i: (0, 0)),
            pl.BlockSpec(memory_space=pl.ANY),
        ],
        out_specs=[hbm, hbm]
        + [pl.BlockSpec((PB_DEV, 2 * EDGE, BS), lambda i: (0, 0, 0))] * groups,
        scratch_shapes=[
            pltpu.VMEM((slots, 2 * CUT, BS), jnp.bfloat16),
            pltpu.VMEM(second.shape, second.dtype),
            pltpu.VMEM(column.shape, column.dtype),
            pltpu.SemaphoreType.DMA((2, UPPER_PARTS)),
            pltpu.SemaphoreType.DMA((4, UPPER_PARTS)),
            pltpu.VMEM((groups * PB_DEV + 1, 2 * EDGE, BS), jnp.float32),
            pltpu.VMEM((2, slots // 2, BS), jnp.float32),
            pltpu.VMEM((2, BS, BS), jnp.float32),
            pltpu.VMEM((pairs, slots, BS), jnp.float32),
            pltpu.VMEM((7, pairs, slots, BS), jnp.float32),
        ],
        out_shape=[second, column]
        + [
            jax.ShapeDtypeStruct(
                (PB_DEV, 2 * EDGE, BS), jnp.float32 if index == 0 else jnp.bfloat16
            )
            for index in range(groups)
        ],
        compiler_params=pltpu.CompilerParams(vmem_limit_bytes=UPPER_VMEM),
        cost_estimate=pl.CostEstimate(
            flops=10**10, bytes_accessed=32 * 2**20, transcendentals=0
        ),
        name="upper_warp",
    )(aims, table, first)


def lower_kernel(pairs, aim_ref, *refs):
    (first, second, row, column), outs = refs[:4], refs[4:-6]
    first_ref, second_ref, row_ref, column_ref, total, arrived = refs[-6:]
    parts = arrived.shape[1]
    per_part = first_ref.shape[0] // parts
    near, far = CUT - REACH, BS - CUT

    def copies(part):
        slots = pl.ds(part * per_part, per_part)
        pieces = [
            (
                first.at[slots, pl.ds(plane * CUT + REACH, near), :],
                first_ref.at[slots, pl.ds(plane * near, near), :],
            )
            for plane in range(2)
        ]
        pieces += [
            (second.at[slots], second_ref.at[slots]),
            (row.at[slots], row_ref.at[slots]),
            (column.at[slots], column_ref.at[slots]),
        ]
        return [
            pltpu.make_async_copy(source, kept, arrived.at[index, part])
            for index, (source, kept) in enumerate(pieces)
        ]

    for part in range(parts):
        for copy in copies(part):
            copy.start()
    total[...] = jnp.zeros_like(total)

    @pl.loop(0, parts)
    def _(part):
        for copy in copies(part):
            copy.wait()
        for inner in range(per_part):
            slot = part * per_part + inner
            source = jnp.concatenate(
                [
                    jnp.concatenate(
                        [
                            first_ref[slot, plane * near : (plane + 1) * near, :],
                            second_ref[slot, plane * far : (plane + 1) * far, :],
                        ],
                        axis=0,
                    )
                    for plane in range(2)
                ],
                axis=1,
            )
            aims = [aim_ref[slot * pairs + pair] for pair in range(pairs)]
            rows = row_ref[slot].reshape(pairs * row_ref.shape[2], BS)[:, : near + far]
            columns = [column_ref[slot, pair] for pair in range(pairs)]
            accumulate(total, aims, rows, source, columns)

    for index, out in enumerate(outs):
        out[...] = total[index * PB_DEV : (index + 1) * PB_DEV].astype(out.dtype)


def lower_warp(aims, first, second, row_maps, column_maps, groups):
    slots, pairs, height, _ = row_maps.shape
    operands = [first, second, row_maps, column_maps]
    return pl.pallas_call(
        functools.partial(lower_kernel, pairs),
        in_specs=[pl.BlockSpec(memory_space=pltpu.SMEM)]
        + [pl.BlockSpec(memory_space=pl.ANY)] * len(operands),
        out_specs=[pl.BlockSpec(memory_space=pltpu.VMEM)] * groups,
        scratch_shapes=[
            pltpu.VMEM((slots, 2 * (CUT - REACH), BS), first.dtype),
            pltpu.VMEM(second.shape, second.dtype),
            pltpu.VMEM(row_maps.shape, row_maps.dtype),
            pltpu.VMEM(column_maps.shape, column_maps.dtype),
            pltpu.VMEM((groups * PB_DEV + 1, 2 * height, BS), jnp.float32),
            pltpu.SemaphoreType.DMA((5, LOWER_PARTS)),
        ],
        out_shape=[
            jax.ShapeDtypeStruct(
                (PB_DEV, 2 * height, BS), jnp.float32 if index == 0 else jnp.bfloat16
            )
            for index in range(groups)
        ],
        compiler_params=pltpu.CompilerParams(vmem_limit_bytes=LOWER_VMEM),
        cost_estimate=pl.CostEstimate(
            flops=6 * 10**9, bytes_accessed=32 * 2**20, transcendentals=0
        ),
        name="lower_warp",
    )(aims, *operands)


def local(
    exposure, variance, pixel_mask, psf_kernel, block_owner, patch_index, pair_stretch, pair_offset
):
    _, rows, columns = exposure.shape
    block_count = columns // BS
    owners = lax.axis_size("sky")
    groups = lax.axis_size("visit")
    slots = owners * CAP
    pairs = patch_index.shape[-1]

    def exchange(array):
        return lax.all_to_all(array, "sky", split_axis=0, concat_axis=0, tiled=True)

    low = jnp.concatenate([exposure[:, rows - HALO :], variance[:, rows - HALO :]], axis=0)
    high = jnp.concatenate([exposure[:, :HALO], variance[:, :HALO]], axis=0)
    top = lax.ppermute(low, "sky", [(i, (i + 1) % owners) for i in range(owners)])
    bottom = lax.ppermute(high, "sky", [((i + 1) % owners, i) for i in range(owners)])

    facts = [
        pair_stretch.transpose(0, 1, 3, 4, 2).reshape(pairs, 2, block_count),
        pair_offset.transpose(0, 1, 3, 4, 2).reshape(pairs, 2, block_count),
        patch_index.transpose(0, 1, 3, 2).reshape(pairs, block_count),
    ]

    images = [array.reshape(rows, columns) for array in (exposure, variance, pixel_mask)]
    common = (owners, block_owner, psf_kernel, images)
    upper_planes = filtered((0, CUT), (0, CUT), *common, "top", top, facts)
    upper_planes, bottom = lax.optimization_barrier((upper_planes, bottom))
    first = exchange(upper_planes)

    lower_planes = filtered((CUT, rows), (CUT, rows), *common, "bottom", bottom)
    first, lower_planes = lax.optimization_barrier((first, lower_planes))
    second = exchange(lower_planes)

    table = first[:, 2 * CUT, :].astype(jnp.float32)
    patch = table[:, 4 * pairs : 5 * pairs].astype(jnp.int32)
    distance = (patch // PB_DEV - lax.axis_index("visit")) % groups
    aims = jnp.where(
        table[:, 5 * pairs : 5 * pairs + 1] > 0.5,
        distance * PB_DEV + patch % PB_DEV,
        groups * PB_DEV,
    )
    aims = aims.reshape(slots * pairs)
    second_maps, column_maps, *upper = upper_warp(aims, table, first, pairs, groups)

    def coadd(sums):
        whole = sums[0]
        for step in (2, 1, 3):
            ring = [(i, (i + step) % groups) for i in range(groups)]
            whole = whole + lax.ppermute(sums[step], "visit", ring).astype(jnp.float32)
        height = whole.shape[1] // 2
        return whole[:, :height] / jnp.maximum(whole[:, height:], 1.0)

    lower = lower_warp(aims, first, second, second_maps, column_maps, groups)
    return jnp.concatenate([coadd(upper), coadd(lower)], axis=1)


def solution(mesh):
    return jax.shard_map(
        local,
        mesh=mesh,
        in_specs=(
            P("visit", "sky", None),
            P("visit", "sky", None),
            P("visit", "sky", None),
            P("visit", None, None),
            P("visit", "sky", None),
            P("visit", "sky", None, None),
            P("visit", "sky", None, None, None),
            P("visit", "sky", None, None, None),
        ),
        out_specs=P(("visit", "sky"), None, None),
        check_vma=False,
    )
```

```python
import functools
import math

import jax
import jax.numpy as jnp
from jax import lax
from jax.experimental import pallas as pl
from jax.experimental.pallas import tpu as pltpu
from jax.sharding import PartitionSpec as P

BS = 128
HALO = 16
BAND = 16
CAP = 2
PB_DEV = 8
FROM, TO = 16, 96
CUT = TO - FROM
BEGIN, END = FROM + 8, TO - 8
EDGE = END - BEGIN
REACH = 16
FACTS = 16
FILTER_COLUMNS = 2048
UNROLL = 2
UPPER_PARTS = 4
FILTER_VMEM = 60 * 1024 * 1024
UPPER_VMEM = 60 * 1024 * 1024
LOWER_VMEM = 58 * 1024 * 1024
LOWER_PARTS = 4


def toeplitz(rows, columns, shift, tap):
    lag = lax.broadcasted_iota(jnp.int32, (rows, columns), 0) - lax.broadcasted_iota(jnp.int32, (rows, columns), 1) + shift
    matrix = jnp.zeros((rows, columns), jnp.float32)
    for index, value in enumerate(tap):
        matrix = jnp.where(lag == index, value, matrix)
    return matrix.astype(jnp.bfloat16)

def segments(spans, rows):
    result, at, frame = [], 0, 0
    for first, last in spans:
        own_from, own_to = max(first - HALO, 0), min(last + HALO, rows)
        own_at = frame + own_from - (first - HALO)
        result.append((first, last, at, frame, own_from, own_to, own_at))
        at += last - first
        frame += last - first + 2 * HALO
    return result, at, frame


def filter_kernel(spans, owners, halo_count, owner_ref, taps_ref, *refs):
    exposure_ref, variance_ref, mask_ref = refs[:3]
    halo_refs = refs[3 : 3 + halo_count]
    pair_refs, out = refs[3 + halo_count : -14], refs[-14]
    framed, usable_ref, across_ref, down_ref, staged, empty_ref, facts_ref = refs[-13:-6]
    slot_ref, count_ref, here, near, done, cleared = refs[-6:]
    rows, columns = mask_ref.shape
    parted, height, tall = segments(spans, rows)
    wide = 2 * BS
    half = (taps_ref.shape[-1] - 1) // 2
    parts = here.shape[1]
    part_columns = columns // parts

    def fetched(part):
        lanes = pl.ds(part * part_columns, part_columns)
        inner = pl.ds(BS + part * part_columns, part_columns)
        pieces = []
        for first, last, at, _, own_from, own_to, own_at in parted:
            own, placed = pl.ds(own_from, own_to - own_from), pl.ds(own_at, own_to - own_from)
            kept, put = pl.ds(first, last - first), pl.ds(at, last - first)
            pieces += [
                (exposure_ref.at[own, lanes], framed.at[0, placed, inner]),
                (variance_ref.at[own, lanes], framed.at[1, placed, inner]),
                (mask_ref.at[kept, lanes], usable_ref.at[put, lanes]),
            ]
        return [
            pltpu.make_async_copy(source, target, here.at[index, part])
            for index, (source, target) in enumerate(pieces)
        ]

    halo_places = (0, tall - HALO)
    halos = [
        pltpu.make_async_copy(
            halo_ref.at[plane],
            framed.at[plane, pl.ds(place, HALO), pl.ds(BS, columns)],
            near.at[index, plane],
        )
        for index, (halo_ref, place) in enumerate(zip(halo_refs, halo_places))
        for plane in range(2)
    ]
    for copy in halos:
        copy.start()
    for part in range(parts):
        for copy in fetched(part):
            copy.start()
    if pair_refs:
        empty_ref[...] = jnp.zeros(empty_ref.shape, jnp.bfloat16)
        clear = pltpu.make_async_copy(
            empty_ref, out.at[:, pl.ds(2 * height, FACTS), :], cleared.at[0]
        )
        clear.start()

    for owner in range(count_ref.shape[0]):
        count_ref[owner] = 0
    for block in range(slot_ref.shape[0]):
        owner = owner_ref[0, 0, block]
        rank = count_ref[owner]
        slot_ref[block] = owner * CAP + rank
        count_ref[owner] = rank + 1

    if pair_refs:
        stretch_ref, offset_ref, patch_ref = pair_refs
        pairs, blocks = patch_ref.shape
        facts_ref[...] = jnp.ones(facts_ref.shape, jnp.float32)
        for pair in range(pairs):
            for base, ref in ((0, stretch_ref), (2 * pairs, offset_ref)):
                facts_ref[base + 2 * pair : base + 2 * pair + 2, :blocks] = ref[pair].astype(
                    jnp.float32
                )
        facts_ref[4 * pairs : 5 * pairs, :blocks] = patch_ref[...].astype(jnp.float32)
        facts_ref[...] = facts_ref[...].T

    margin = jnp.zeros((tall, BS), jnp.bfloat16)
    empty = jnp.zeros((BS, BS), jnp.bfloat16)
    values = taps_ref[0].astype(jnp.float32)
    for plane in range(2):
        framed[plane, :, :BS] = margin
        framed[plane, :, BS + columns :] = margin
        taps = [
            [values[way : way + 1, tap : tap + 1] for tap in range(taps_ref.shape[-1])]
            for way in range(2)
        ]
        if plane == 1:
            taps = [[tap * tap for tap in way] for way in taps]
        left, middle, right = (toeplitz(BS, BS, half + by * BS, taps[0]) for by in (-1, 0, 1))
        pattern = ((left, empty), (middle, left), (right, middle), (empty, right))
        for row, blocks in enumerate(pattern):
            across_ref[plane, row * BS : (row + 1) * BS, :BS] = blocks[0]
            across_ref[plane, row * BS : (row + 1) * BS, BS:] = blocks[1]
        place = lax.broadcasted_iota(jnp.int32, (height, tall), 0)
        shift = jnp.full((height, tall), half + HALO, jnp.int32)
        for _, _, at, frame, *_ in parted[1:]:
            shift = jnp.where(place >= at, half + HALO + frame - at, shift)
        down_ref[plane] = toeplitz(height, tall, shift, taps[1][::-1])

    for copy in halos:
        copy.wait()
    for place, outermost in list(zip(halo_places, (0, owners - 1)))[:halo_count]:
        inner = lax.axis_index("sky") != outermost
        for plane in range(2):
            halo = framed[plane, place : place + HALO, :]
            framed[plane, place : place + HALO, :] = jnp.where(inner, halo, jnp.zeros_like(halo))
    for copy in fetched(0):
        copy.wait()
    tiles = part_columns // wide
    sent = []
    for part in range(parts):
        if part + 1 < parts:
            for copy in fetched(part + 1):
                copy.wait()
        base = part * part_columns
        matched = []
        for plane in range(2):
            stack = jnp.concatenate(
                [
                    framed[plane, :, base + tile * wide : base + tile * wide + 4 * BS]
                    for tile in range(tiles)
                ],
                axis=0,
            )
            passed = jnp.dot(
                stack, across_ref[plane], preferred_element_type=jnp.float32
            ).astype(jnp.bfloat16)
            matched.append(
                [
                    jnp.dot(
                        down_ref[plane],
                        passed[tile * tall : (tile + 1) * tall],
                        preferred_element_type=jnp.float32,
                    )
                    for tile in range(tiles)
                ]
            )
        for tile in range(tiles):
            lanes = slice(base + tile * wide, base + (tile + 1) * wide)
            weight = usable_ref[:, lanes].astype(jnp.float32) / matched[1][tile]
            weighted = (weight * matched[0][tile]).astype(jnp.bfloat16)
            weight = weight.astype(jnp.bfloat16)
            for block in range(2):
                index = (part * tiles + tile) * 2 + block
                lanes = slice(block * BS, (block + 1) * BS)
                staged[index, :height, :] = weighted[:, lanes]
                staged[index, height : 2 * height, :] = weight[:, lanes]
                if pair_refs:
                    row = jnp.broadcast_to(facts_ref[index : index + 1, :], (FACTS, BS))
                    staged[index, 2 * height :, :] = row.astype(jnp.bfloat16)
        if pair_refs and part == 0:
            clear.wait()
        for index in range(part * tiles * 2, (part + 1) * tiles * 2):
            copy = pltpu.make_async_copy(
                staged.at[index], out.at[slot_ref[index]], done.at[index]
            )
            copy.start()
            sent.append(copy)
    for copy in sent:
        copy.wait()


def filtered(spans, owners, owner, taps, images, halos=(), facts=()):
    rows, columns = images[2].shape
    _, height, frame = segments(spans, rows)
    tall = 2 * height + (FACTS if facts else 0)
    slots = owners * CAP
    blocks = columns // BS
    parts = columns // FILTER_COLUMNS
    smem = pl.BlockSpec(memory_space=pltpu.SMEM)
    hbm = pl.BlockSpec(memory_space=pltpu.HBM)

    def whole(array):
        return pl.BlockSpec(array.shape, lambda i: (0,) * array.ndim)

    operands = [owner, taps, *images, *halos, *facts]
    specs = [smem, whole(taps), hbm, hbm, hbm] + [pl.BlockSpec(memory_space=pl.ANY)] * len(halos)
    specs += [whole(fact) for fact in facts]
    return pl.pallas_call(
        functools.partial(filter_kernel, spans, owners, len(halos)),
        grid=(1,),
        out_shape=jax.ShapeDtypeStruct((slots, tall, BS), jnp.bfloat16),
        in_specs=specs,
        out_specs=hbm,
        scratch_shapes=[
            pltpu.VMEM((2, frame, columns + 2 * BS), jnp.bfloat16),
            pltpu.VMEM((height, columns), jnp.int32),
            pltpu.VMEM((2, 4 * BS, 2 * BS), jnp.bfloat16),
            pltpu.VMEM((2, height, frame), jnp.bfloat16),
            pltpu.VMEM((blocks, tall, BS), jnp.bfloat16),
            pltpu.VMEM((slots, FACTS, BS), jnp.bfloat16),
            pltpu.VMEM((BS, BS), jnp.float32),
            pltpu.SMEM((blocks,), jnp.int32),
            pltpu.SMEM((owners,), jnp.int32),
            pltpu.SemaphoreType.DMA((3 * len(spans), parts)),
            pltpu.SemaphoreType.DMA((2, 2)),
            pltpu.SemaphoreType.DMA((blocks,)),
            pltpu.SemaphoreType.DMA((1,)),
        ],
        compiler_params=pltpu.CompilerParams(vmem_limit_bytes=FILTER_VMEM),
        cost_estimate=pl.CostEstimate(
            flops=2 * 10**9, bytes_accessed=16 * 2**20, transcendentals=0
        ),
        name="filter",
    )(*operands)


def series(square, count, odd):
    total = jnp.zeros_like(square)
    for term in range(count, -1, -1):
        total = total * square + (-1.0) ** term / math.factorial(2 * term + odd)
    return total


def accumulate(total, aims, rows, source, columns):
    height = rows.shape[0] // len(columns)
    half_warp = jnp.dot(rows, source, preferred_element_type=jnp.float32).astype(jnp.bfloat16)
    for pair, column in enumerate(columns):
        mine = half_warp[pair * height : (pair + 1) * height]
        both = jnp.concatenate([mine[:, :BS], mine[:, BS:]], axis=0)
        total[aims[pair]] += jnp.dot(both, column, preferred_element_type=jnp.float32)


def upper_kernel(pairs, aim_ref, table_ref, first_ref, second_out, column_out, *refs):
    outs, (block_ref, second_ref, column_ref, arrived, left) = refs[:-10], refs[-10:-5]
    total, spread_ref, place_ref, near_ref, taps_ref = refs[-5:]
    parts = arrived.shape[1]
    half = table_ref.shape[0] // 2
    per_part = half // parts
    lanes = lax.broadcasted_iota(jnp.int32, (BS, BS), 1)
    rows = lax.broadcasted_iota(jnp.int32, (BS, BS), 0)
    group = lanes // BAND
    centre = (BS - 1) / 2.0

    def fetched(part):
        return [
            pltpu.make_async_copy(
                first_ref.at[pl.ds(base + part * per_part, per_part), pl.ds(0, 2 * CUT), :],
                block_ref.at[pl.ds(base + part * per_part, per_part)],
                arrived.at[index, part],
            )
            for index, base in enumerate((0, half))
        ]

    def returned(part):
        return [
            pltpu.make_async_copy(
                kept.at[pl.ds(base + part * per_part, per_part)],
                out.at[pl.ds(base + part * per_part, per_part)],
                left.at[2 * kind + index, part],
            )
            for index, base in enumerate((0, half))
            for kind, (kept, out) in enumerate(((second_ref, second_out), (column_ref, column_out)))
        ]

    for part in range(parts):
        for copy in fetched(part):
            copy.start()
    total[...] = jnp.zeros_like(total)
    target = rows + lanes % BAND - BAND // 2
    inside = (target >= 0) & (target < BS)
    place_ref[0] = rows.astype(jnp.float32) - centre
    place_ref[1] = jnp.where(inside, target.astype(jnp.float32) - centre, 1e3)

    facts = table_ref[...].astype(jnp.bfloat16)

    def sent(values, chosen):
        return jnp.dot(values, chosen.astype(jnp.bfloat16), preferred_element_type=jnp.float32)

    for kind in range(2):
        field = 2 * pairs * kind
        spread_ref[kind] = sent(
            facts[:half], (rows == field + 2 * group) & (group < pairs)
        ) + sent(facts[half:], (rows == field + 2 * (group - pairs)) & (group >= pairs))
    pixels = lanes[: 2 * half].astype(jnp.float32) - centre
    for pair in range(pairs):
        stretch = sent(facts, rows == 2 * pair + 1)
        offset = sent(facts, rows == 2 * pairs + 2 * pair + 1)
        source = (1.0 + stretch) * pixels + centre + offset
        near = jnp.round(source)
        x = source - near
        near_ref[pair] = near
        whole, third = math.pi * x, (math.pi / 3.0) * x
        whole_sinc = series(whole * whole, 8, 1)
        third_sinc = series(third * third, 8, 1)
        third_cos = series(third * third, 8, 0)
        for k in range(-3, 4):
            if k == 0:
                value = whole_sinc * third_sinc
            else:
                angle = math.pi * k / 3.0
                slow = third_sinc * third * math.cos(angle) - third_cos * math.sin(angle)
                far = x - k
                value = ((-1.0) ** k * 3.0 / math.pi**2) * whole_sinc * whole * slow / (far * far)
                value = jnp.where(jnp.abs(far) < 3.0, value, 0.0)
            taps_ref[k + 3, pair] = value

    numbers = rows.astype(jnp.bfloat16)

    def build(m):
        stretch = spread_ref[0, pl.ds(m, 1), :]
        offset = spread_ref[1, pl.ds(m, 1), :]
        x = (1.0 + stretch) * place_ref[0] + offset - place_ref[1]
        square = x * x * (math.pi / 3.0) ** 2
        power = series(square, 10, 1)
        power = power * power
        value = power * (1.0 - (4.0 / 3.0) * power * square)
        value = jnp.where(jnp.abs(x) < 3.0, value, 0.0)
        for which in range(2):
            slot = m + which * half
            stack, columns = [], []
            for pair in range(pairs):
                index = which * pairs + pair
                one = jnp.where(group == index, value, 0.0)
                shift = -BAND // 2 - BAND * index
                inner, above, below = (
                    pltpu.roll(
                        one[begin:end], (shift + begin - lane) % BS, 1, stride=1, stride_axis=0
                    )
                    for begin, end, lane in (
                        (BEGIN, END, FROM),
                        (0, BEGIN, 0),
                        (END, BS, TO - FROM - 2 * REACH),
                    )
                )
                second_ref[slot, pair] = jnp.concatenate([above, below], axis=0).astype(
                    jnp.bfloat16
                )
                stack.append(inner.astype(jnp.bfloat16)[:, :CUT])
                lag = numbers - near_ref[pair, pl.ds(slot, 1), :].astype(jnp.bfloat16)
                column = jnp.zeros((BS, BS), jnp.bfloat16)
                for k in range(7):
                    tap = taps_ref[k, pair, pl.ds(slot, 1), :].astype(jnp.bfloat16)
                    column = jnp.where(lag == jnp.bfloat16(k - 3), tap, column)
                column_ref[slot, pair] = column
                columns.append(column)
            source = jnp.concatenate(
                [block_ref[slot, :CUT, :], block_ref[slot, CUT : 2 * CUT, :]], axis=1
            )
            aims = [aim_ref[slot * pairs + pair] for pair in range(pairs)]
            accumulate(total, aims, jnp.concatenate(stack, axis=0), source, columns)

    @pl.loop(0, parts)
    def _(part):
        for copy in fetched(part):
            copy.wait()

        @pl.loop(0, per_part // UNROLL)
        def _(batch):
            for inner in range(UNROLL):
                build(part * per_part + batch * UNROLL + inner)

        for copy in returned(part):
            copy.start()

    for index, out in enumerate(outs):
        out[...] = total[index * PB_DEV : (index + 1) * PB_DEV].astype(out.dtype)
    for part in range(parts):
        for copy in returned(part):
            copy.wait()


def upper_warp(aims, table, first, pairs, groups):
    slots = first.shape[0]
    second = jax.ShapeDtypeStruct((slots, pairs, BS - EDGE, BS), jnp.bfloat16)
    column = jax.ShapeDtypeStruct((slots, pairs, BS, BS), jnp.bfloat16)
    hbm = pl.BlockSpec(memory_space=pltpu.HBM)
    return pl.pallas_call(
        functools.partial(upper_kernel, pairs),
        grid=(1,),
        in_specs=[
            pl.BlockSpec(memory_space=pltpu.SMEM),
            pl.BlockSpec(table.shape, lambda i: (0, 0)),
            pl.BlockSpec(memory_space=pl.ANY),
        ],
        out_specs=[hbm, hbm]
        + [pl.BlockSpec((PB_DEV, 2 * EDGE, BS), lambda i: (0, 0, 0))] * groups,
        scratch_shapes=[
            pltpu.VMEM((slots, 2 * CUT, BS), jnp.bfloat16),
            pltpu.VMEM(second.shape, second.dtype),
            pltpu.VMEM(column.shape, column.dtype),
            pltpu.SemaphoreType.DMA((2, UPPER_PARTS)),
            pltpu.SemaphoreType.DMA((4, UPPER_PARTS)),
            pltpu.VMEM((groups * PB_DEV + 1, 2 * EDGE, BS), jnp.float32),
            pltpu.VMEM((2, slots // 2, BS), jnp.float32),
            pltpu.VMEM((2, BS, BS), jnp.float32),
            pltpu.VMEM((pairs, slots, BS), jnp.float32),
            pltpu.VMEM((7, pairs, slots, BS), jnp.float32),
        ],
        out_shape=[second, column]
        + [
            jax.ShapeDtypeStruct(
                (PB_DEV, 2 * EDGE, BS), jnp.float32 if index == 0 else jnp.bfloat16
            )
            for index in range(groups)
        ],
        compiler_params=pltpu.CompilerParams(vmem_limit_bytes=UPPER_VMEM),
        cost_estimate=pl.CostEstimate(
            flops=10**10, bytes_accessed=32 * 2**20, transcendentals=0
        ),
        name="upper_warp",
    )(aims, table, first)


def lower_kernel(pairs, aim_ref, *refs):
    (first, second, row, column), outs = refs[:4], refs[4:-6]
    first_ref, second_ref, row_ref, column_ref, total, arrived = refs[-6:]
    parts = arrived.shape[1]
    per_part = first_ref.shape[0] // parts
    far = BS - CUT

    def copies(part):
        slots = pl.ds(part * per_part, per_part)
        pieces = [
            (
                first.at[slots, pl.ds(begin, count), :],
                first_ref.at[slots, pl.ds(place, count), :],
            )
            for begin, count, place in (
                (0, REACH, 0),
                (CUT - REACH, 2 * REACH, REACH),
                (2 * CUT - REACH, REACH, 3 * REACH),
            )
        ]
        pieces += [
            (second.at[slots], second_ref.at[slots]),
            (row.at[slots], row_ref.at[slots]),
            (column.at[slots], column_ref.at[slots]),
        ]
        return [
            pltpu.make_async_copy(source, kept, arrived.at[index, part])
            for index, (source, kept) in enumerate(pieces)
        ]

    for part in range(parts):
        for copy in copies(part):
            copy.start()
    total[...] = jnp.zeros_like(total)

    @pl.loop(0, parts)
    def _(part):
        for copy in copies(part):
            copy.wait()
        for inner in range(per_part):
            slot = part * per_part + inner
            source = jnp.concatenate(
                [
                    jnp.concatenate(
                        [
                            second_ref[slot, plane * far : plane * far + FROM, :],
                            first_ref[slot, plane * 2 * REACH : (plane + 1) * 2 * REACH, :],
                            second_ref[slot, plane * far + FROM : (plane + 1) * far, :],
                        ],
                        axis=0,
                    )
                    for plane in range(2)
                ],
                axis=1,
            )
            aims = [aim_ref[slot * pairs + pair] for pair in range(pairs)]
            rows = row_ref[slot].reshape(pairs * row_ref.shape[2], BS)[:, : 2 * REACH + far]
            columns = [column_ref[slot, pair] for pair in range(pairs)]
            accumulate(total, aims, rows, source, columns)

    for index, out in enumerate(outs):
        out[...] = total[index * PB_DEV : (index + 1) * PB_DEV].astype(out.dtype)


def lower_warp(aims, first, second, row_maps, column_maps, groups):
    slots, pairs, height, _ = row_maps.shape
    operands = [first, second, row_maps, column_maps]
    return pl.pallas_call(
        functools.partial(lower_kernel, pairs),
        in_specs=[pl.BlockSpec(memory_space=pltpu.SMEM)]
        + [pl.BlockSpec(memory_space=pl.ANY)] * len(operands),
        out_specs=[pl.BlockSpec(memory_space=pltpu.VMEM)] * groups,
        scratch_shapes=[
            pltpu.VMEM((slots, 4 * REACH, BS), first.dtype),
            pltpu.VMEM(second.shape, second.dtype),
            pltpu.VMEM(row_maps.shape, row_maps.dtype),
            pltpu.VMEM(column_maps.shape, column_maps.dtype),
            pltpu.VMEM((groups * PB_DEV + 1, 2 * height, BS), jnp.float32),
            pltpu.SemaphoreType.DMA((6, LOWER_PARTS)),
        ],
        out_shape=[
            jax.ShapeDtypeStruct(
                (PB_DEV, 2 * height, BS), jnp.float32 if index == 0 else jnp.bfloat16
            )
            for index in range(groups)
        ],
        compiler_params=pltpu.CompilerParams(vmem_limit_bytes=LOWER_VMEM),
        cost_estimate=pl.CostEstimate(
            flops=6 * 10**9, bytes_accessed=32 * 2**20, transcendentals=0
        ),
        name="lower_warp",
    )(aims, *operands)


def local(
    exposure, variance, pixel_mask, psf_kernel, block_owner, patch_index, pair_stretch, pair_offset
):
    _, rows, columns = exposure.shape
    block_count = columns // BS
    owners = lax.axis_size("sky")
    groups = lax.axis_size("visit")
    slots = owners * CAP
    pairs = patch_index.shape[-1]

    def exchange(array):
        return lax.all_to_all(array, "sky", split_axis=0, concat_axis=0, tiled=True)

    low = jnp.concatenate([exposure[:, rows - HALO :], variance[:, rows - HALO :]], axis=0)
    high = jnp.concatenate([exposure[:, :HALO], variance[:, :HALO]], axis=0)
    top = lax.ppermute(low, "sky", [(i, (i + 1) % owners) for i in range(owners)])
    bottom = lax.ppermute(high, "sky", [((i + 1) % owners, i) for i in range(owners)])

    facts = [
        pair_stretch.transpose(0, 1, 3, 4, 2).reshape(pairs, 2, block_count),
        pair_offset.transpose(0, 1, 3, 4, 2).reshape(pairs, 2, block_count),
        patch_index.transpose(0, 1, 3, 2).reshape(pairs, block_count),
    ]

    images = [array.reshape(rows, columns) for array in (exposure, variance, pixel_mask)]
    common = (owners, block_owner, psf_kernel, images)
    inner_planes = filtered([(FROM, TO)], *common, facts=facts)
    inner_planes, top, bottom = lax.optimization_barrier((inner_planes, top, bottom))
    first = exchange(inner_planes)

    outer_planes = filtered([(0, FROM), (TO, rows)], *common, halos=(top, bottom))
    first, outer_planes = lax.optimization_barrier((first, outer_planes))
    second = exchange(outer_planes)

    table = first[:, 2 * CUT, :].astype(jnp.float32)
    patch = table[:, 4 * pairs : 5 * pairs].astype(jnp.int32)
    distance = (patch // PB_DEV) ^ lax.axis_index("visit")
    aims = jnp.where(
        table[:, 5 * pairs : 5 * pairs + 1] > 0.5,
        distance * PB_DEV + patch % PB_DEV,
        groups * PB_DEV,
    )
    aims = aims.reshape(slots * pairs)
    second_maps, column_maps, *upper = upper_warp(aims, table, first, pairs, groups)

    def coadd(sums):
        whole = sums[0]
        for step in (2, 1, 3):
            ring = [(i, i ^ step) for i in range(groups)]
            whole = whole + lax.ppermute(sums[step], "visit", ring).astype(jnp.float32)
        height = whole.shape[1] // 2
        return whole[:, :height] / jnp.maximum(whole[:, height:], 1.0)

    lower = lower_warp(aims, first, second, second_maps, column_maps, groups)
    inner, outer = coadd(upper), coadd(lower)
    return jnp.concatenate([outer[:, :BEGIN], inner, outer[:, BEGIN:]], axis=1)


def solution(mesh):
    return jax.shard_map(
        local,
        mesh=mesh,
        in_specs=(
            P("visit", "sky", None),
            P("visit", "sky", None),
            P("visit", "sky", None),
            P("visit", None, None),
            P("visit", "sky", None),
            P("visit", "sky", None, None),
            P("visit", "sky", None, None, None),
            P("visit", "sky", None, None, None),
        ),
        out_specs=P(("visit", "sky"), None, None),
        check_vma=False,
    )
```

```python
import functools
import math

import jax
import jax.numpy as jnp
from jax import lax
from jax.experimental import pallas as pl
from jax.experimental.pallas import tpu as pltpu
from jax.sharding import PartitionSpec as P

BS = 128
HALO = 16
BAND = 16
CAP = 2
PB_DEV = 8
FROM, TO = 16, 96
CUT = TO - FROM
BEGIN, END = FROM + 8, TO - 8
EDGE = END - BEGIN
REACH = 16
FACTS = 8
FILTER_COLUMNS = 2048
UPPER_PARTS = 4
FILTER_VMEM = 60 * 1024 * 1024
UPPER_VMEM = 60 * 1024 * 1024
LOWER_VMEM = 58 * 1024 * 1024
LOWER_PARTS = 4


def toeplitz(rows, columns, shift, tap):
    lag = lax.broadcasted_iota(jnp.int32, (rows, columns), 0) - lax.broadcasted_iota(jnp.int32, (rows, columns), 1) + shift
    matrix = jnp.zeros((rows, columns), jnp.float32)
    for index, value in enumerate(tap):
        matrix = jnp.where(lag == index, value, matrix)
    return matrix.astype(jnp.bfloat16)

def segments(spans, rows):
    result, at, frame = [], 0, 0
    for first, last in spans:
        own_from, own_to = max(first - HALO, 0), min(last + HALO, rows)
        own_at = frame + own_from - (first - HALO)
        result.append((first, last, at, frame, own_from, own_to, own_at))
        at += last - first
        frame += last - first + 2 * HALO
    return result, at, frame


def filter_kernel(spans, owners, halo_count, owner_ref, taps_ref, *refs):
    exposure_ref, variance_ref, mask_ref = refs[:3]
    halo_refs = refs[3 : 3 + halo_count]
    pair_refs, out = refs[3 + halo_count : -15], refs[-15]
    framed, usable_ref, across_ref, down_ref, staged, facts_ref, known_ref, told_ref = refs[-14:-6]
    slot_ref, count_ref, here, near, done, cleared = refs[-6:]
    rows, columns = mask_ref.shape
    parted, height, tall = segments(spans, rows)
    wide = 2 * BS
    half = (taps_ref.shape[-1] - 1) // 2
    parts = here.shape[1]
    part_columns = columns // parts

    def fetched(part):
        lanes = pl.ds(part * part_columns, part_columns)
        inner = pl.ds(BS + part * part_columns, part_columns)
        pieces = []
        for first, last, at, _, own_from, own_to, own_at in parted:
            own, placed = pl.ds(own_from, own_to - own_from), pl.ds(own_at, own_to - own_from)
            kept, put = pl.ds(first, last - first), pl.ds(at, last - first)
            pieces += [
                (exposure_ref.at[own, lanes], framed.at[0, placed, inner]),
                (variance_ref.at[own, lanes], framed.at[1, placed, inner]),
                (mask_ref.at[kept, lanes], usable_ref.at[put, lanes]),
            ]
        return [
            pltpu.make_async_copy(source, target, here.at[index, part])
            for index, (source, target) in enumerate(pieces)
        ]

    halo_places = (0, tall - HALO)
    halos = [
        pltpu.make_async_copy(
            halo_ref.at[plane],
            framed.at[plane, pl.ds(place, HALO), pl.ds(BS, columns)],
            near.at[index, plane],
        )
        for index, (halo_ref, place) in enumerate(zip(halo_refs, halo_places))
        for plane in range(2)
    ]
    for copy in halos:
        copy.start()
    for part in range(parts):
        for copy in fetched(part):
            copy.start()

    for owner in range(count_ref.shape[0]):
        count_ref[owner] = 0
    for block in range(slot_ref.shape[0]):
        owner = owner_ref[0, 0, block]
        rank = count_ref[owner]
        slot_ref[block] = owner * CAP + rank
        count_ref[owner] = rank + 1

    sent = []
    if pair_refs:
        stretch_ref, offset_ref, patch_ref = pair_refs
        pairs, blocks = patch_ref.shape
        facts_ref[...] = jnp.ones(facts_ref.shape, jnp.float32)
        for pair in range(pairs):
            for base, ref in ((0, stretch_ref), (2 * pairs, offset_ref)):
                facts_ref[base + 2 * pair : base + 2 * pair + 2, :blocks] = ref[pair].astype(
                    jnp.float32
                )
        facts_ref[4 * pairs : 5 * pairs, :blocks] = patch_ref[...].astype(jnp.float32)
        facts_ref[...] = facts_ref[...].T
        known_ref[...] = jnp.zeros(known_ref.shape, jnp.float32)
        for block in range(blocks):
            slot = slot_ref[block]
            begin = pl.multiple_of((slot % CAP) * FACTS, FACTS)
            known_ref[slot // CAP, pl.ds(begin, FACTS), :] = jnp.broadcast_to(
                facts_ref[block : block + 1, :], (FACTS, BS)
            )
        told_ref[...] = known_ref[...].astype(jnp.bfloat16)
        tell = pltpu.make_async_copy(
            told_ref, out.at[:, pl.ds(2 * CAP * height, CAP * FACTS), :], cleared.at[0]
        )
        tell.start()
        sent.append(tell)

    margin = jnp.zeros((tall, BS), jnp.bfloat16)
    empty = jnp.zeros((BS, BS), jnp.bfloat16)
    values = taps_ref[0].astype(jnp.float32)
    for plane in range(2):
        framed[plane, :, :BS] = margin
        framed[plane, :, BS + columns :] = margin
        taps = [
            [values[way : way + 1, tap : tap + 1] for tap in range(taps_ref.shape[-1])]
            for way in range(2)
        ]
        if plane == 1:
            taps = [[tap * tap for tap in way] for way in taps]
        left, middle, right = (toeplitz(BS, BS, half + by * BS, taps[0]) for by in (-1, 0, 1))
        pattern = ((left, empty), (middle, left), (right, middle), (empty, right))
        for row, blocks in enumerate(pattern):
            across_ref[plane, row * BS : (row + 1) * BS, :BS] = blocks[0]
            across_ref[plane, row * BS : (row + 1) * BS, BS:] = blocks[1]
        place = lax.broadcasted_iota(jnp.int32, (height, tall), 0)
        shift = jnp.full((height, tall), half + HALO, jnp.int32)
        for _, _, at, frame, *_ in parted[1:]:
            shift = jnp.where(place >= at, half + HALO + frame - at, shift)
        down_ref[plane] = toeplitz(height, tall, shift, taps[1][::-1])

    for copy in halos:
        copy.wait()
    for place, outermost in list(zip(halo_places, (0, owners - 1)))[:halo_count]:
        inner = lax.axis_index("sky") != outermost
        for plane in range(2):
            halo = framed[plane, place : place + HALO, :]
            framed[plane, place : place + HALO, :] = jnp.where(inner, halo, jnp.zeros_like(halo))
    for copy in fetched(0):
        copy.wait()
    tiles = part_columns // wide
    for part in range(parts):
        if part + 1 < parts:
            for copy in fetched(part + 1):
                copy.wait()
        base = part * part_columns
        matched = []
        for plane in range(2):
            stack = jnp.concatenate(
                [
                    framed[plane, :, base + tile * wide : base + tile * wide + 4 * BS]
                    for tile in range(tiles)
                ],
                axis=0,
            )
            passed = jnp.dot(
                stack, across_ref[plane], preferred_element_type=jnp.float32
            ).astype(jnp.bfloat16)
            matched.append(
                [
                    jnp.dot(
                        down_ref[plane],
                        passed[tile * tall : (tile + 1) * tall],
                        preferred_element_type=jnp.float32,
                    )
                    for tile in range(tiles)
                ]
            )
        for tile in range(tiles):
            lanes = slice(base + tile * wide, base + (tile + 1) * wide)
            weight = usable_ref[:, lanes].astype(jnp.float32) / matched[1][tile]
            weighted = (weight * matched[0][tile]).astype(jnp.bfloat16)
            weight = weight.astype(jnp.bfloat16)
            for block in range(2):
                index = (part * tiles + tile) * 2 + block
                lanes = slice(block * BS, (block + 1) * BS)
                staged[index, :height, :] = weighted[:, lanes]
                staged[index, height : 2 * height, :] = weight[:, lanes]
        for index in range(part * tiles * 2, (part + 1) * tiles * 2):
            copy = pltpu.make_async_copy(
                staged.at[index],
                out.at[
                    slot_ref[index] // CAP,
                    pl.ds(pl.multiple_of((slot_ref[index] % CAP) * 2 * height, HALO), 2 * height),
                    :,
                ],
                done.at[index],
            )
            copy.start()
            sent.append(copy)
    for copy in sent:
        copy.wait()


def filtered(spans, owners, owner, taps, images, halos=(), facts=()):
    rows, columns = images[2].shape
    _, height, frame = segments(spans, rows)
    tall = CAP * (2 * height + (FACTS if facts else 0))
    blocks = columns // BS
    parts = columns // FILTER_COLUMNS
    smem = pl.BlockSpec(memory_space=pltpu.SMEM)
    hbm = pl.BlockSpec(memory_space=pltpu.HBM)

    def whole(array):
        return pl.BlockSpec(array.shape, lambda i: (0,) * array.ndim)

    operands = [owner, taps, *images, *halos, *facts]
    specs = [smem, whole(taps), hbm, hbm, hbm] + [pl.BlockSpec(memory_space=pl.ANY)] * len(halos)
    specs += [whole(fact) for fact in facts]
    return pl.pallas_call(
        functools.partial(filter_kernel, spans, owners, len(halos)),
        grid=(1,),
        out_shape=jax.ShapeDtypeStruct((owners, tall, BS), jnp.bfloat16),
        in_specs=specs,
        out_specs=hbm,
        scratch_shapes=[
            pltpu.VMEM((2, frame, columns + 2 * BS), jnp.bfloat16),
            pltpu.VMEM((height, columns), jnp.int32),
            pltpu.VMEM((2, 4 * BS, 2 * BS), jnp.bfloat16),
            pltpu.VMEM((2, height, frame), jnp.bfloat16),
            pltpu.VMEM((blocks, 2 * height, BS), jnp.bfloat16),
            pltpu.VMEM((BS, BS), jnp.float32),
            pltpu.VMEM((owners, CAP * FACTS, BS), jnp.float32),
            pltpu.VMEM((owners, CAP * FACTS, BS), jnp.bfloat16),
            pltpu.SMEM((blocks,), jnp.int32),
            pltpu.SMEM((owners,), jnp.int32),
            pltpu.SemaphoreType.DMA((3 * len(spans), parts)),
            pltpu.SemaphoreType.DMA((2, 2)),
            pltpu.SemaphoreType.DMA((blocks,)),
            pltpu.SemaphoreType.DMA((1,)),
        ],
        compiler_params=pltpu.CompilerParams(vmem_limit_bytes=FILTER_VMEM),
        cost_estimate=pl.CostEstimate(
            flops=2 * 10**9, bytes_accessed=16 * 2**20, transcendentals=0
        ),
        name="filter",
    )(*operands)


def series(square, count, odd):
    total = jnp.zeros_like(square)
    for term in range(count, -1, -1):
        total = total * square + (-1.0) ** term / math.factorial(2 * term + odd)
    return total


def accumulate(total, aims, rows, source, columns):
    height = rows.shape[0] // len(columns)
    half_warp = jnp.dot(rows, source, preferred_element_type=jnp.float32).astype(jnp.bfloat16)
    for pair, column in enumerate(columns):
        mine = half_warp[pair * height : (pair + 1) * height]
        both = jnp.concatenate([mine[:, :BS], mine[:, BS:]], axis=0)
        total[aims[pair]] += jnp.dot(both, column, preferred_element_type=jnp.float32)


def upper_kernel(pairs, aim_ref, table_ref, first_ref, second_out, column_out, *refs):
    outs, (block_ref, second_ref, column_ref, arrived, left) = refs[:-10], refs[-10:-5]
    total, spread_ref, place_ref, near_ref, taps_ref = refs[-5:]
    parts = arrived.shape[1]
    half = table_ref.shape[0] // 2
    per_part = half // parts
    lanes = lax.broadcasted_iota(jnp.int32, (BS, BS), 1)
    rows = lax.broadcasted_iota(jnp.int32, (BS, BS), 0)
    group = lanes // BAND
    centre = (BS - 1) / 2.0

    def fetched(part):
        return [
            pltpu.make_async_copy(
                first_ref.at[
                    pl.ds((base + part * per_part) // CAP, per_part // CAP),
                    pl.ds(0, 2 * CAP * CUT),
                    :,
                ],
                block_ref.at[pl.ds((base + part * per_part) // CAP, per_part // CAP)],
                arrived.at[index, part],
            )
            for index, base in enumerate((0, half))
        ]

    def returned(part):
        return [
            pltpu.make_async_copy(
                kept.at[pl.ds(base + part * per_part, per_part)],
                out.at[pl.ds(base + part * per_part, per_part)],
                left.at[2 * kind + index, part],
            )
            for index, base in enumerate((0, half))
            for kind, (kept, out) in enumerate(((second_ref, second_out), (column_ref, column_out)))
        ]

    for part in range(parts):
        for copy in fetched(part):
            copy.start()
    total[...] = jnp.zeros_like(total)
    target = rows + lanes % BAND - BAND // 2
    inside = (target >= 0) & (target < BS)
    place_ref[0] = rows.astype(jnp.float32) - centre
    place_ref[1] = jnp.where(inside, target.astype(jnp.float32) - centre, 1e3)

    facts = table_ref[...].astype(jnp.bfloat16)

    def sent(values, chosen):
        return jnp.dot(values, chosen.astype(jnp.bfloat16), preferred_element_type=jnp.float32)

    for kind in range(2):
        field = 2 * pairs * kind
        spread_ref[kind] = sent(
            facts[:half], (rows == field + 2 * group) & (group < pairs)
        ) + sent(facts[half:], (rows == field + 2 * (group - pairs)) & (group >= pairs))
    pixels = lanes[: 2 * half].astype(jnp.float32) - centre
    for pair in range(pairs):
        stretch = sent(facts, rows == 2 * pair + 1)
        offset = sent(facts, rows == 2 * pairs + 2 * pair + 1)
        source = (1.0 + stretch) * pixels + centre + offset
        near = jnp.round(source)
        x = source - near
        near_ref[pair] = near
        whole, third = math.pi * x, (math.pi / 3.0) * x
        whole_sinc = series(whole * whole, 8, 1)
        third_sinc = series(third * third, 8, 1)
        third_cos = series(third * third, 8, 0)
        for k in range(-3, 4):
            if k == 0:
                value = whole_sinc * third_sinc
            else:
                angle = math.pi * k / 3.0
                slow = third_sinc * third * math.cos(angle) - third_cos * math.sin(angle)
                far = x - k
                value = ((-1.0) ** k * 3.0 / math.pi**2) * whole_sinc * whole * slow / (far * far)
                value = jnp.where(jnp.abs(far) < 3.0, value, 0.0)
            taps_ref[k + 3, pair] = value

    numbers = rows.astype(jnp.bfloat16)

    def build(owner, rank):
        m = owner * CAP + rank
        stretch = spread_ref[0, pl.ds(m, 1), :]
        offset = spread_ref[1, pl.ds(m, 1), :]
        x = (1.0 + stretch) * place_ref[0] + offset - place_ref[1]
        square = x * x * (math.pi / 3.0) ** 2
        power = series(square, 10, 1)
        power = power * power
        value = power * (1.0 - (4.0 / 3.0) * power * square)
        value = jnp.where(jnp.abs(x) < 3.0, value, 0.0)
        for which in range(2):
            slot = m + which * half
            stack, columns = [], []
            for pair in range(pairs):
                index = which * pairs + pair
                one = jnp.where(group == index, value, 0.0)
                shift = -BAND // 2 - BAND * index
                inner, above, below = (
                    pltpu.roll(
                        one[begin:end], (shift + begin - lane) % BS, 1, stride=1, stride_axis=0
                    )
                    for begin, end, lane in (
                        (BEGIN, END, FROM),
                        (0, BEGIN, 0),
                        (END, BS, TO - FROM - 2 * REACH),
                    )
                )
                second_ref[slot, pair] = jnp.concatenate([above, below], axis=0).astype(
                    jnp.bfloat16
                )
                stack.append(inner.astype(jnp.bfloat16)[:, :CUT])
                lag = numbers - near_ref[pair, pl.ds(slot, 1), :].astype(jnp.bfloat16)
                column = jnp.zeros((BS, BS), jnp.bfloat16)
                for k in range(7):
                    tap = taps_ref[k, pair, pl.ds(slot, 1), :].astype(jnp.bfloat16)
                    column = jnp.where(lag == jnp.bfloat16(k - 3), tap, column)
                column_ref[slot, pair] = column
                columns.append(column)
            holder, base = owner + which * (half // CAP), rank * 2 * CUT
            source = jnp.concatenate(
                [
                    block_ref[holder, base : base + CUT, :],
                    block_ref[holder, base + CUT : base + 2 * CUT, :],
                ],
                axis=1,
            )
            aims = [aim_ref[slot * pairs + pair] for pair in range(pairs)]
            accumulate(total, aims, jnp.concatenate(stack, axis=0), source, columns)

    @pl.loop(0, parts)
    def _(part):
        for copy in fetched(part):
            copy.wait()

        @pl.loop(0, per_part // CAP)
        def _(owner):
            for rank in range(CAP):
                build(part * (per_part // CAP) + owner, rank)

        for copy in returned(part):
            copy.start()

    for index, out in enumerate(outs):
        out[...] = total[index * PB_DEV : (index + 1) * PB_DEV].astype(out.dtype)
    for part in range(parts):
        for copy in returned(part):
            copy.wait()


def upper_warp(aims, table, first, pairs, groups):
    slots = first.shape[0] * CAP
    second = jax.ShapeDtypeStruct((slots, pairs, BS - EDGE, BS), jnp.bfloat16)
    column = jax.ShapeDtypeStruct((slots, pairs, BS, BS), jnp.bfloat16)
    hbm = pl.BlockSpec(memory_space=pltpu.HBM)
    return pl.pallas_call(
        functools.partial(upper_kernel, pairs),
        grid=(1,),
        in_specs=[
            pl.BlockSpec(memory_space=pltpu.SMEM),
            pl.BlockSpec(table.shape, lambda i: (0, 0)),
            pl.BlockSpec(memory_space=pl.ANY),
        ],
        out_specs=[hbm, hbm]
        + [pl.BlockSpec((PB_DEV, 2 * EDGE, BS), lambda i: (0, 0, 0))] * groups,
        scratch_shapes=[
            pltpu.VMEM((slots // CAP, 2 * CAP * CUT, BS), jnp.bfloat16),
            pltpu.VMEM(second.shape, second.dtype),
            pltpu.VMEM(column.shape, column.dtype),
            pltpu.SemaphoreType.DMA((2, UPPER_PARTS)),
            pltpu.SemaphoreType.DMA((4, UPPER_PARTS)),
            pltpu.VMEM((groups * PB_DEV + 1, 2 * EDGE, BS), jnp.float32),
            pltpu.VMEM((2, slots // 2, BS), jnp.float32),
            pltpu.VMEM((2, BS, BS), jnp.float32),
            pltpu.VMEM((pairs, slots, BS), jnp.float32),
            pltpu.VMEM((7, pairs, slots, BS), jnp.float32),
        ],
        out_shape=[second, column]
        + [
            jax.ShapeDtypeStruct(
                (PB_DEV, 2 * EDGE, BS), jnp.float32 if index == 0 else jnp.bfloat16
            )
            for index in range(groups)
        ],
        compiler_params=pltpu.CompilerParams(vmem_limit_bytes=UPPER_VMEM),
        cost_estimate=pl.CostEstimate(
            flops=10**10, bytes_accessed=32 * 2**20, transcendentals=0
        ),
        name="upper_warp",
    )(aims, table, first)


def lower_kernel(pairs, aim_ref, *refs):
    (first, second, row, column), outs = refs[:4], refs[4:-6]
    first_ref, second_ref, row_ref, column_ref, total, arrived = refs[-6:]
    parts = arrived.shape[1]
    per_part = row_ref.shape[0] // parts
    far = BS - CUT

    def copies(part):
        slots = pl.ds(part * per_part, per_part)
        holders = pl.ds(part * per_part // CAP, per_part // CAP)
        pieces = [
            (
                first.at[holders, pl.ds(rank * 2 * CUT + begin, count), :],
                first_ref.at[holders, pl.ds(rank * 4 * REACH + place, count), :],
            )
            for rank in range(CAP)
            for begin, count, place in (
                (0, REACH, 0),
                (CUT - REACH, 2 * REACH, REACH),
                (2 * CUT - REACH, REACH, 3 * REACH),
            )
        ]
        pieces += [
            (second.at[holders], second_ref.at[holders]),
            (row.at[slots], row_ref.at[slots]),
            (column.at[slots], column_ref.at[slots]),
        ]
        return [
            pltpu.make_async_copy(source, kept, arrived.at[index, part])
            for index, (source, kept) in enumerate(pieces)
        ]

    for part in range(parts):
        for copy in copies(part):
            copy.start()
    total[...] = jnp.zeros_like(total)

    @pl.loop(0, parts)
    def _(part):
        for copy in copies(part):
            copy.wait()
        for inner in range(per_part):
            slot = part * per_part + inner
            holder = part * (per_part // CAP) + inner // CAP
            near_at, far_at = (inner % CAP) * 4 * REACH, (inner % CAP) * 2 * far
            source = jnp.concatenate(
                [
                    jnp.concatenate(
                        [
                            second_ref[holder, begin : begin + FROM, :],
                            first_ref[holder, near : near + 2 * REACH, :],
                            second_ref[holder, begin + FROM : begin + far, :],
                        ],
                        axis=0,
                    )
                    for near, begin in (
                        (near_at, far_at),
                        (near_at + 2 * REACH, far_at + far),
                    )
                ],
                axis=1,
            )
            aims = [aim_ref[slot * pairs + pair] for pair in range(pairs)]
            rows = row_ref[slot].reshape(pairs * row_ref.shape[2], BS)[:, : 2 * REACH + far]
            columns = [column_ref[slot, pair] for pair in range(pairs)]
            accumulate(total, aims, rows, source, columns)

    for index, out in enumerate(outs):
        out[...] = total[index * PB_DEV : (index + 1) * PB_DEV].astype(out.dtype)


def lower_warp(aims, first, second, row_maps, column_maps, groups):
    slots, pairs, height, _ = row_maps.shape
    operands = [first, second, row_maps, column_maps]
    return pl.pallas_call(
        functools.partial(lower_kernel, pairs),
        in_specs=[pl.BlockSpec(memory_space=pltpu.SMEM)]
        + [pl.BlockSpec(memory_space=pl.ANY)] * len(operands),
        out_specs=[pl.BlockSpec(memory_space=pltpu.VMEM)] * groups,
        scratch_shapes=[
            pltpu.VMEM((slots // CAP, 4 * CAP * REACH, BS), first.dtype),
            pltpu.VMEM(second.shape, second.dtype),
            pltpu.VMEM(row_maps.shape, row_maps.dtype),
            pltpu.VMEM(column_maps.shape, column_maps.dtype),
            pltpu.VMEM((groups * PB_DEV + 1, 2 * height, BS), jnp.float32),
            pltpu.SemaphoreType.DMA((3 * CAP + 3, LOWER_PARTS)),
        ],
        out_shape=[
            jax.ShapeDtypeStruct(
                (PB_DEV, 2 * height, BS), jnp.float32 if index == 0 else jnp.bfloat16
            )
            for index in range(groups)
        ],
        compiler_params=pltpu.CompilerParams(vmem_limit_bytes=LOWER_VMEM),
        cost_estimate=pl.CostEstimate(
            flops=6 * 10**9, bytes_accessed=32 * 2**20, transcendentals=0
        ),
        name="lower_warp",
    )(aims, *operands)


def local(
    exposure, variance, pixel_mask, psf_kernel, block_owner, patch_index, pair_stretch, pair_offset
):
    _, rows, columns = exposure.shape
    block_count = columns // BS
    owners = lax.axis_size("sky")
    groups = lax.axis_size("visit")
    slots = owners * CAP
    pairs = patch_index.shape[-1]

    def exchange(array):
        return lax.all_to_all(array, "sky", split_axis=0, concat_axis=0, tiled=True)

    low = jnp.concatenate([exposure[:, rows - HALO :], variance[:, rows - HALO :]], axis=0)
    high = jnp.concatenate([exposure[:, :HALO], variance[:, :HALO]], axis=0)
    top = lax.ppermute(low, "sky", [(i, (i + 1) % owners) for i in range(owners)])
    bottom = lax.ppermute(high, "sky", [((i + 1) % owners, i) for i in range(owners)])

    facts = [
        pair_stretch.transpose(0, 1, 3, 4, 2).reshape(pairs, 2, block_count),
        pair_offset.transpose(0, 1, 3, 4, 2).reshape(pairs, 2, block_count),
        patch_index.transpose(0, 1, 3, 2).reshape(pairs, block_count),
    ]

    images = [array.reshape(rows, columns) for array in (exposure, variance, pixel_mask)]
    common = (owners, block_owner, psf_kernel, images)
    inner_planes = filtered([(FROM, TO)], *common, facts=facts)
    inner_planes, top, bottom = lax.optimization_barrier((inner_planes, top, bottom))
    first = exchange(inner_planes)

    outer_planes = filtered([(0, FROM), (TO, rows)], *common, halos=(top, bottom))
    first, outer_planes = lax.optimization_barrier((first, outer_planes))
    second = exchange(outer_planes)

    table = first[:, 2 * CAP * CUT :: FACTS, :].astype(jnp.float32).reshape(slots, BS)
    patch = table[:, 4 * pairs : 5 * pairs].astype(jnp.int32)
    distance = (patch // PB_DEV) ^ lax.axis_index("visit")
    aims = jnp.where(
        table[:, 5 * pairs : 5 * pairs + 1] > 0.5,
        distance * PB_DEV + patch % PB_DEV,
        groups * PB_DEV,
    )
    aims = aims.reshape(slots * pairs)
    second_maps, column_maps, *upper = upper_warp(aims, table, first, pairs, groups)

    def coadd(sums):
        whole = sums[0]
        for step in (2, 1, 3):
            ring = [(i, i ^ step) for i in range(groups)]
            whole = whole + lax.ppermute(sums[step], "visit", ring).astype(jnp.float32)
        height = whole.shape[1] // 2
        return whole[:, :height] / jnp.maximum(whole[:, height:], 1.0)

    lower = lower_warp(aims, first, second, second_maps, column_maps, groups)
    inner, outer = coadd(upper), coadd(lower)
    return jnp.concatenate([outer[:, :BEGIN], inner, outer[:, BEGIN:]], axis=1)


def solution(mesh):
    return jax.shard_map(
        local,
        mesh=mesh,
        in_specs=(
            P("visit", "sky", None),
            P("visit", "sky", None),
            P("visit", "sky", None),
            P("visit", None, None),
            P("visit", "sky", None),
            P("visit", "sky", None, None),
            P("visit", "sky", None, None, None),
            P("visit", "sky", None, None, None),
        ),
        out_specs=P(("visit", "sky"), None, None),
        check_vma=False,
    )
```

```python
import functools
import math

import jax
import jax.numpy as jnp
from jax import lax
from jax.experimental import pallas as pl
from jax.experimental.pallas import tpu as pltpu
from jax.sharding import PartitionSpec as P

BS = 128
HALO = 16
BAND = 16
CAP = 2
PB_DEV = 8
FROM, TO = 16, 96
CUT = TO - FROM
BEGIN, END = FROM + 8, TO - 8
EDGE = END - BEGIN
REACH = 16
FACTS = 8
FILTER_COLUMNS = 2048
UPPER_PARTS = 4
FILTER_VMEM = 60 * 1024 * 1024
UPPER_VMEM = 60 * 1024 * 1024
LOWER_VMEM = 58 * 1024 * 1024
LOWER_PARTS = 4


def toeplitz(rows, columns, shift, tap):
    lag = lax.broadcasted_iota(jnp.int32, (rows, columns), 0) - lax.broadcasted_iota(jnp.int32, (rows, columns), 1) + shift
    matrix = jnp.zeros((rows, columns), jnp.float32)
    for index, value in enumerate(tap):
        matrix = jnp.where(lag == index, value, matrix)
    return matrix.astype(jnp.bfloat16)

def segments(spans, rows):
    result, at, frame = [], 0, 0
    for first, last in spans:
        own_from, own_to = max(first - HALO, 0), min(last + HALO, rows)
        own_at = frame + own_from - (first - HALO)
        result.append((first, last, at, frame, own_from, own_to, own_at))
        at += last - first
        frame += last - first + 2 * HALO
    return result, at, frame


def filter_kernel(spans, owners, halo_count, owner_ref, taps_ref, *refs):
    exposure_ref, variance_ref, mask_ref = refs[:3]
    halo_refs = refs[3 : 3 + halo_count]
    pair_refs, out = refs[3 + halo_count : -15], refs[-15]
    framed, usable_ref, across_ref, down_ref, staged, facts_ref, known_ref, told_ref = refs[-14:-6]
    slot_ref, count_ref, here, near, done, cleared = refs[-6:]
    rows, columns = mask_ref.shape
    parted, height, tall = segments(spans, rows)
    wide = 2 * BS
    half = (taps_ref.shape[-1] - 1) // 2
    parts = here.shape[1]
    part_columns = columns // parts

    def fetched(part):
        lanes = pl.ds(part * part_columns, part_columns)
        inner = pl.ds(BS + part * part_columns, part_columns)
        pieces = []
        for first, last, at, _, own_from, own_to, own_at in parted:
            own, placed = pl.ds(own_from, own_to - own_from), pl.ds(own_at, own_to - own_from)
            kept, put = pl.ds(first, last - first), pl.ds(at, last - first)
            pieces += [
                (exposure_ref.at[own, lanes], framed.at[0, placed, inner]),
                (variance_ref.at[own, lanes], framed.at[1, placed, inner]),
                (mask_ref.at[kept, lanes], usable_ref.at[put, lanes]),
            ]
        return [
            pltpu.make_async_copy(source, target, here.at[index, part])
            for index, (source, target) in enumerate(pieces)
        ]

    halo_places = (0, tall - HALO)
    halos = [
        pltpu.make_async_copy(
            halo_ref.at[plane],
            framed.at[plane, pl.ds(place, HALO), pl.ds(BS, columns)],
            near.at[index, plane],
        )
        for index, (halo_ref, place) in enumerate(zip(halo_refs, halo_places))
        for plane in range(2)
    ]
    for copy in halos:
        copy.start()
    for part in range(parts):
        for copy in fetched(part):
            copy.start()

    for owner in range(count_ref.shape[0]):
        count_ref[owner] = 0
    for block in range(slot_ref.shape[0]):
        owner = owner_ref[0, 0, block]
        rank = count_ref[owner]
        slot_ref[block] = owner * CAP + rank
        count_ref[owner] = rank + 1

    sent = []
    if pair_refs:
        stretch_ref, offset_ref, patch_ref = pair_refs
        pairs, blocks = patch_ref.shape
        facts_ref[...] = jnp.ones(facts_ref.shape, jnp.float32)
        for pair in range(pairs):
            for base, ref in ((0, stretch_ref), (2 * pairs, offset_ref)):
                facts_ref[base + 2 * pair : base + 2 * pair + 2, :blocks] = ref[pair].astype(
                    jnp.float32
                )
        facts_ref[4 * pairs : 5 * pairs, :blocks] = patch_ref[...].astype(jnp.float32)
        facts_ref[...] = facts_ref[...].T
        known_ref[...] = jnp.zeros(known_ref.shape, jnp.float32)
        for block in range(blocks):
            slot = slot_ref[block]
            begin = pl.multiple_of((slot % CAP) * FACTS, FACTS)
            known_ref[slot // CAP, pl.ds(begin, FACTS), :] = jnp.broadcast_to(
                facts_ref[block : block + 1, :], (FACTS, BS)
            )
        told_ref[...] = known_ref[...].astype(jnp.bfloat16)
        tell = pltpu.make_async_copy(
            told_ref, out.at[:, pl.ds(2 * CAP * height, CAP * FACTS), :], cleared.at[0]
        )
        tell.start()
        sent.append(tell)

    margin = jnp.zeros((tall, BS), jnp.bfloat16)
    empty = jnp.zeros((BS, BS), jnp.bfloat16)
    values = taps_ref[0].astype(jnp.float32)
    for plane in range(2):
        framed[plane, :, :BS] = margin
        framed[plane, :, BS + columns :] = margin
        taps = [
            [values[way : way + 1, tap : tap + 1] for tap in range(taps_ref.shape[-1])]
            for way in range(2)
        ]
        if plane == 1:
            taps = [[tap * tap for tap in way] for way in taps]
        left, middle, right = (toeplitz(BS, BS, half + by * BS, taps[0]) for by in (-1, 0, 1))
        pattern = ((left, empty), (middle, left), (right, middle), (empty, right))
        for row, blocks in enumerate(pattern):
            across_ref[plane, row * BS : (row + 1) * BS, :BS] = blocks[0]
            across_ref[plane, row * BS : (row + 1) * BS, BS:] = blocks[1]
        place = lax.broadcasted_iota(jnp.int32, (height, tall), 0)
        shift = jnp.full((height, tall), half + HALO, jnp.int32)
        for _, _, at, frame, *_ in parted[1:]:
            shift = jnp.where(place >= at, half + HALO + frame - at, shift)
        down_ref[plane] = toeplitz(height, tall, shift, taps[1][::-1])

    for copy in halos:
        copy.wait()
    for place, outermost in list(zip(halo_places, (0, owners - 1)))[:halo_count]:
        inner = lax.axis_index("sky") != outermost
        for plane in range(2):
            halo = framed[plane, place : place + HALO, :]
            framed[plane, place : place + HALO, :] = jnp.where(inner, halo, jnp.zeros_like(halo))
    for copy in fetched(0):
        copy.wait()
    tiles = part_columns // wide
    for part in range(parts):
        if part + 1 < parts:
            for copy in fetched(part + 1):
                copy.wait()
        base = part * part_columns
        matched = []
        for plane in range(2):
            stack = jnp.concatenate(
                [
                    framed[plane, :, base + tile * wide : base + tile * wide + 4 * BS]
                    for tile in range(tiles)
                ],
                axis=0,
            )
            passed = jnp.dot(
                stack, across_ref[plane], preferred_element_type=jnp.float32
            ).astype(jnp.bfloat16)
            matched.append(
                [
                    jnp.dot(
                        down_ref[plane],
                        passed[tile * tall : (tile + 1) * tall],
                        preferred_element_type=jnp.float32,
                    )
                    for tile in range(tiles)
                ]
            )
        for tile in range(tiles):
            lanes = slice(base + tile * wide, base + (tile + 1) * wide)
            weight = usable_ref[:, lanes].astype(jnp.float32) / matched[1][tile]
            weighted = (weight * matched[0][tile]).astype(jnp.bfloat16)
            weight = weight.astype(jnp.bfloat16)
            for block in range(2):
                index = (part * tiles + tile) * 2 + block
                lanes = slice(block * BS, (block + 1) * BS)
                staged[index, :height, :] = weighted[:, lanes]
                staged[index, height : 2 * height, :] = weight[:, lanes]
        for index in range(part * tiles * 2, (part + 1) * tiles * 2):
            copy = pltpu.make_async_copy(
                staged.at[index],
                out.at[
                    slot_ref[index] // CAP,
                    pl.ds(pl.multiple_of((slot_ref[index] % CAP) * 2 * height, HALO), 2 * height),
                    :,
                ],
                done.at[index],
            )
            copy.start()
            sent.append(copy)
    for copy in sent:
        copy.wait()


def filtered(spans, owners, owner, taps, images, halos=(), facts=()):
    rows, columns = images[2].shape
    _, height, frame = segments(spans, rows)
    tall = CAP * (2 * height + (FACTS if facts else 0))
    blocks = columns // BS
    parts = columns // FILTER_COLUMNS
    smem = pl.BlockSpec(memory_space=pltpu.SMEM)
    hbm = pl.BlockSpec(memory_space=pltpu.HBM)

    def whole(array):
        return pl.BlockSpec(array.shape, lambda i: (0,) * array.ndim)

    operands = [owner, taps, *images, *halos, *facts]
    specs = [smem, whole(taps), hbm, hbm, hbm] + [pl.BlockSpec(memory_space=pl.ANY)] * len(halos)
    specs += [whole(fact) for fact in facts]
    return pl.pallas_call(
        functools.partial(filter_kernel, spans, owners, len(halos)),
        grid=(1,),
        out_shape=jax.ShapeDtypeStruct((owners, tall, BS), jnp.bfloat16),
        in_specs=specs,
        out_specs=hbm,
        scratch_shapes=[
            pltpu.VMEM((2, frame, columns + 2 * BS), jnp.bfloat16),
            pltpu.VMEM((height, columns), jnp.int32),
            pltpu.VMEM((2, 4 * BS, 2 * BS), jnp.bfloat16),
            pltpu.VMEM((2, height, frame), jnp.bfloat16),
            pltpu.VMEM((blocks, 2 * height, BS), jnp.bfloat16),
            pltpu.VMEM((BS, BS), jnp.float32),
            pltpu.VMEM((owners, CAP * FACTS, BS), jnp.float32),
            pltpu.VMEM((owners, CAP * FACTS, BS), jnp.bfloat16),
            pltpu.SMEM((blocks,), jnp.int32),
            pltpu.SMEM((owners,), jnp.int32),
            pltpu.SemaphoreType.DMA((3 * len(spans), parts)),
            pltpu.SemaphoreType.DMA((2, 2)),
            pltpu.SemaphoreType.DMA((blocks,)),
            pltpu.SemaphoreType.DMA((1,)),
        ],
        compiler_params=pltpu.CompilerParams(vmem_limit_bytes=FILTER_VMEM),
        cost_estimate=pl.CostEstimate(
            flops=2 * 10**9, bytes_accessed=16 * 2**20, transcendentals=0
        ),
        name="filter",
    )(*operands)


def series(square, count, odd):
    total = jnp.zeros_like(square)
    for term in range(count, -1, -1):
        total = total * square + (-1.0) ** term / math.factorial(2 * term + odd)
    return total


def accumulate(total, aims, rows, source, columns):
    height = rows.shape[0] // len(columns)
    half_warp = jnp.dot(rows, source, preferred_element_type=jnp.float32).astype(jnp.bfloat16)
    for pair, column in enumerate(columns):
        mine = half_warp[pair * height : (pair + 1) * height]
        both = jnp.concatenate([mine[:, :BS], mine[:, BS:]], axis=0)
        total[aims[pair]] += jnp.dot(both, column, preferred_element_type=jnp.float32)


def upper_kernel(pairs, aim_ref, table_ref, first_ref, second_out, column_out, *refs):
    outs, (block_ref, second_ref, column_ref, arrived, left) = refs[:-10], refs[-10:-5]
    total, spread_ref, place_ref, near_ref, taps_ref = refs[-5:]
    parts = arrived.shape[1]
    half = table_ref.shape[0] // 2
    per_part = half // parts
    lanes = lax.broadcasted_iota(jnp.int32, (BS, BS), 1)
    rows = lax.broadcasted_iota(jnp.int32, (BS, BS), 0)
    group = lanes // BAND
    centre = (BS - 1) / 2.0

    def fetched(part):
        return [
            pltpu.make_async_copy(
                first_ref.at[
                    pl.ds((base + part * per_part) // CAP, per_part // CAP),
                    pl.ds(0, 2 * CAP * CUT),
                    :,
                ],
                block_ref.at[pl.ds((base + part * per_part) // CAP, per_part // CAP)],
                arrived.at[index, part],
            )
            for index, base in enumerate((0, half))
        ]

    def returned(part):
        return [
            pltpu.make_async_copy(
                kept.at[pl.ds(base + part * per_part, per_part)],
                out.at[pl.ds(base + part * per_part, per_part)],
                left.at[2 * kind + index, part],
            )
            for index, base in enumerate((0, half))
            for kind, (kept, out) in enumerate(((second_ref, second_out), (column_ref, column_out)))
        ]

    for part in range(parts):
        for copy in fetched(part):
            copy.start()
    total[...] = jnp.zeros_like(total)
    target = rows + lanes % BAND - BAND // 2
    inside = (target >= 0) & (target < BS)
    place_ref[0] = rows.astype(jnp.float32) - centre
    place_ref[1] = jnp.where(inside, target.astype(jnp.float32) - centre, 1e3)

    facts = table_ref[...].astype(jnp.bfloat16)

    def sent(values, chosen):
        return jnp.dot(values, chosen.astype(jnp.bfloat16), preferred_element_type=jnp.float32)

    for kind in range(2):
        field = 2 * pairs * kind
        spread_ref[kind] = sent(
            facts[:half], (rows == field + 2 * group) & (group < pairs)
        ) + sent(facts[half:], (rows == field + 2 * (group - pairs)) & (group >= pairs))
    pixels = lanes[: 2 * half].astype(jnp.float32) - centre
    for pair in range(pairs):
        stretch = sent(facts, rows == 2 * pair + 1)
        offset = sent(facts, rows == 2 * pairs + 2 * pair + 1)
        source = (1.0 + stretch) * pixels + centre + offset
        near = jnp.round(source)
        x = source - near
        near_ref[pair] = near
        whole, third = math.pi * x, (math.pi / 3.0) * x
        whole_sinc = series(whole * whole, 8, 1)
        third_sinc = series(third * third, 8, 1)
        third_cos = series(third * third, 8, 0)
        for k in range(-3, 4):
            if k == 0:
                value = whole_sinc * third_sinc
            else:
                angle = math.pi * k / 3.0
                slow = third_sinc * third * math.cos(angle) - third_cos * math.sin(angle)
                far = x - k
                value = ((-1.0) ** k * 3.0 / math.pi**2) * whole_sinc * whole * slow / (far * far)
                value = jnp.where(jnp.abs(far) < 3.0, value, 0.0)
            taps_ref[k + 3, pair] = value

    numbers = rows.astype(jnp.bfloat16)

    def build(owner, rank):
        m = owner * CAP + rank
        stretch = spread_ref[0, pl.ds(m, 1), :]
        offset = spread_ref[1, pl.ds(m, 1), :]
        x = (1.0 + stretch) * place_ref[0] + offset - place_ref[1]
        square = x * x * (math.pi / 3.0) ** 2
        power = series(square, 10, 1)
        power = power * power
        value = power * (1.0 - (4.0 / 3.0) * power * square)
        value = jnp.where(jnp.abs(x) < 3.0, value, 0.0)
        for which in range(2):
            slot = m + which * half
            stack, columns = [], []
            for pair in range(pairs):
                index = which * pairs + pair
                one = jnp.where(group == index, value, 0.0)
                shift = -BAND // 2 - BAND * index
                inner, above, below = (
                    pltpu.roll(
                        one[begin:end], (shift + begin - lane) % BS, 1, stride=1, stride_axis=0
                    )
                    for begin, end, lane in (
                        (BEGIN, END, FROM),
                        (0, BEGIN, 0),
                        (END, BS, TO - FROM - 2 * REACH),
                    )
                )
                second_ref[slot, pair] = jnp.concatenate([above, below], axis=0).astype(
                    jnp.bfloat16
                )
                stack.append(inner.astype(jnp.bfloat16)[:, :CUT])
                lag = numbers - near_ref[pair, pl.ds(slot, 1), :].astype(jnp.bfloat16)
                column = jnp.zeros((BS, BS), jnp.bfloat16)
                for k in range(7):
                    tap = taps_ref[k, pair, pl.ds(slot, 1), :].astype(jnp.bfloat16)
                    column = jnp.where(lag == jnp.bfloat16(k - 3), tap, column)
                column_ref[slot, pair] = column
                columns.append(column)
            holder, base = owner + which * (half // CAP), rank * 2 * CUT
            source = jnp.concatenate(
                [
                    block_ref[holder, base : base + CUT, :],
                    block_ref[holder, base + CUT : base + 2 * CUT, :],
                ],
                axis=1,
            )
            aims = [aim_ref[slot * pairs + pair] for pair in range(pairs)]
            accumulate(total, aims, jnp.concatenate(stack, axis=0), source, columns)

    @pl.loop(0, parts)
    def _(part):
        for copy in fetched(part):
            copy.wait()

        @pl.loop(0, per_part // CAP)
        def _(owner):
            for rank in range(CAP):
                build(part * (per_part // CAP) + owner, rank)

        for copy in returned(part):
            copy.start()

    for index, out in enumerate(outs):
        out[...] = total[index * PB_DEV : (index + 1) * PB_DEV].astype(out.dtype)
    for part in range(parts):
        for copy in returned(part):
            copy.wait()


def upper_warp(aims, table, first, pairs, groups):
    slots = first.shape[0] * CAP
    second = jax.ShapeDtypeStruct((slots, pairs, BS - EDGE, BS), jnp.bfloat16)
    column = jax.ShapeDtypeStruct((slots, pairs, BS, BS), jnp.bfloat16)
    hbm = pl.BlockSpec(memory_space=pltpu.HBM)
    return pl.pallas_call(
        functools.partial(upper_kernel, pairs),
        grid=(1,),
        in_specs=[
            pl.BlockSpec(memory_space=pltpu.SMEM),
            pl.BlockSpec(table.shape, lambda i: (0, 0)),
            pl.BlockSpec(memory_space=pl.ANY),
        ],
        out_specs=[hbm, hbm]
        + [pl.BlockSpec((PB_DEV, 2 * EDGE, BS), lambda i: (0, 0, 0))] * groups,
        scratch_shapes=[
            pltpu.VMEM((slots // CAP, 2 * CAP * CUT, BS), jnp.bfloat16),
            pltpu.VMEM(second.shape, second.dtype),
            pltpu.VMEM(column.shape, column.dtype),
            pltpu.SemaphoreType.DMA((2, UPPER_PARTS)),
            pltpu.SemaphoreType.DMA((4, UPPER_PARTS)),
            pltpu.VMEM((groups * PB_DEV + 1, 2 * EDGE, BS), jnp.float32),
            pltpu.VMEM((2, slots // 2, BS), jnp.float32),
            pltpu.VMEM((2, BS, BS), jnp.float32),
            pltpu.VMEM((pairs, slots, BS), jnp.float32),
            pltpu.VMEM((7, pairs, slots, BS), jnp.float32),
        ],
        out_shape=[second, column]
        + [
            jax.ShapeDtypeStruct(
                (PB_DEV, 2 * EDGE, BS), jnp.float32 if index == 0 else jnp.bfloat16
            )
            for index in range(groups)
        ],
        compiler_params=pltpu.CompilerParams(vmem_limit_bytes=UPPER_VMEM),
        cost_estimate=pl.CostEstimate(
            flops=10**10, bytes_accessed=32 * 2**20, transcendentals=0
        ),
        name="upper_warp",
    )(aims, table, first)


def lower_kernel(pairs, aim_ref, *refs):
    (first, second, row, column), outs = refs[:4], refs[4:-6]
    first_ref, second_ref, row_ref, column_ref, total, arrived = refs[-6:]
    parts = arrived.shape[1]
    per_part = row_ref.shape[0] // parts
    far = BS - CUT

    def copies(part):
        slots = pl.ds(part * per_part, per_part)
        holders = pl.ds(part * per_part // CAP, per_part // CAP)
        pieces = [
            (
                first.at[holders, pl.ds(rank * 2 * CUT + begin, count), :],
                first_ref.at[holders, pl.ds(rank * 4 * REACH + place, count), :],
            )
            for rank in range(CAP)
            for begin, count, place in (
                (0, REACH, 0),
                (CUT - REACH, 2 * REACH, REACH),
                (2 * CUT - REACH, REACH, 3 * REACH),
            )
        ]
        pieces += [
            (second.at[holders], second_ref.at[holders]),
            (row.at[slots], row_ref.at[slots]),
            (column.at[slots], column_ref.at[slots]),
        ]
        return [
            pltpu.make_async_copy(source, kept, arrived.at[index, part])
            for index, (source, kept) in enumerate(pieces)
        ]

    for part in range(parts):
        for copy in copies(part):
            copy.start()
    total[...] = jnp.zeros_like(total)

    @pl.loop(0, parts)
    def _(part):
        for copy in copies(part):
            copy.wait()
        for inner in range(per_part):
            slot = part * per_part + inner
            holder = part * (per_part // CAP) + inner // CAP
            near_at, far_at = (inner % CAP) * 4 * REACH, (inner % CAP) * 2 * far
            source = jnp.concatenate(
                [
                    jnp.concatenate(
                        [
                            second_ref[holder, begin : begin + FROM, :],
                            first_ref[holder, near : near + 2 * REACH, :],
                            second_ref[holder, begin + FROM : begin + far, :],
                        ],
                        axis=0,
                    )
                    for near, begin in (
                        (near_at, far_at),
                        (near_at + 2 * REACH, far_at + far),
                    )
                ],
                axis=1,
            )
            aims = [aim_ref[slot * pairs + pair] for pair in range(pairs)]
            rows = row_ref[slot].reshape(pairs * row_ref.shape[2], BS)[:, : 2 * REACH + far]
            columns = [column_ref[slot, pair] for pair in range(pairs)]
            accumulate(total, aims, rows, source, columns)

    for index, out in enumerate(outs):
        out[...] = total[index * PB_DEV : (index + 1) * PB_DEV].astype(out.dtype)


def lower_warp(aims, first, second, row_maps, column_maps, groups):
    slots, pairs, height, _ = row_maps.shape
    operands = [first, second, row_maps, column_maps]
    return pl.pallas_call(
        functools.partial(lower_kernel, pairs),
        in_specs=[pl.BlockSpec(memory_space=pltpu.SMEM)]
        + [pl.BlockSpec(memory_space=pl.ANY)] * len(operands),
        out_specs=[pl.BlockSpec(memory_space=pltpu.VMEM)] * groups,
        scratch_shapes=[
            pltpu.VMEM((slots // CAP, 4 * CAP * REACH, BS), first.dtype),
            pltpu.VMEM(second.shape, second.dtype),
            pltpu.VMEM(row_maps.shape, row_maps.dtype),
            pltpu.VMEM(column_maps.shape, column_maps.dtype),
            pltpu.VMEM((groups * PB_DEV + 1, 2 * height, BS), jnp.float32),
            pltpu.SemaphoreType.DMA((3 * CAP + 3, LOWER_PARTS)),
        ],
        out_shape=[
            jax.ShapeDtypeStruct(
                (PB_DEV, 2 * height, BS), jnp.float32 if index == 0 else jnp.bfloat16
            )
            for index in range(groups)
        ],
        compiler_params=pltpu.CompilerParams(vmem_limit_bytes=LOWER_VMEM),
        cost_estimate=pl.CostEstimate(
            flops=6 * 10**9, bytes_accessed=32 * 2**20, transcendentals=0
        ),
        name="lower_warp",
    )(aims, *operands)


def local(
    exposure, variance, pixel_mask, psf_kernel, block_owner, patch_index, pair_stretch, pair_offset
):
    _, rows, columns = exposure.shape
    block_count = columns // BS
    owners = lax.axis_size("sky")
    groups = lax.axis_size("visit")
    slots = owners * CAP
    pairs = patch_index.shape[-1]

    def exchange(array):
        return lax.all_to_all(array, "sky", split_axis=0, concat_axis=0, tiled=True)

    low = jnp.concatenate([exposure[:, rows - HALO :], variance[:, rows - HALO :]], axis=0)
    high = jnp.concatenate([exposure[:, :HALO], variance[:, :HALO]], axis=0)
    even = lax.axis_index("sky") % 2 == 0
    near = lax.ppermute(
        jnp.where(even, low, high), "sky", [(i, i ^ 1) for i in range(owners)]
    )
    far = lax.ppermute(
        jnp.where(even, high, low),
        "sky",
        [(i, (i - 1 if i % 2 == 0 else i + 1) % owners) for i in range(owners)],
    )

    facts = [
        pair_stretch.transpose(0, 1, 3, 4, 2).reshape(pairs, 2, block_count),
        pair_offset.transpose(0, 1, 3, 4, 2).reshape(pairs, 2, block_count),
        patch_index.transpose(0, 1, 3, 2).reshape(pairs, block_count),
    ]

    images = [array.reshape(rows, columns) for array in (exposure, variance, pixel_mask)]
    common = (owners, block_owner, psf_kernel, images)
    inner_planes = filtered([(FROM, TO)], *common, facts=facts)
    inner_planes, near, far = lax.optimization_barrier((inner_planes, near, far))
    first = exchange(inner_planes)

    top, bottom = jnp.where(even, far, near), jnp.where(even, near, far)
    outer_planes = filtered([(0, FROM), (TO, rows)], *common, halos=(top, bottom))
    first, outer_planes = lax.optimization_barrier((first, outer_planes))
    second = exchange(outer_planes)

    table = first[:, 2 * CAP * CUT :: FACTS, :].astype(jnp.float32).reshape(slots, BS)
    patch = table[:, 4 * pairs : 5 * pairs].astype(jnp.int32)
    distance = (patch // PB_DEV) ^ lax.axis_index("visit")
    aims = jnp.where(
        table[:, 5 * pairs : 5 * pairs + 1] > 0.5,
        distance * PB_DEV + patch % PB_DEV,
        groups * PB_DEV,
    )
    aims = aims.reshape(slots * pairs)
    second_maps, column_maps, *upper = upper_warp(aims, table, first, pairs, groups)

    def coadd(sums):
        whole = sums[0]
        for step in (2, 1, 3):
            ring = [(i, i ^ step) for i in range(groups)]
            whole = whole + lax.ppermute(sums[step], "visit", ring).astype(jnp.float32)
        height = whole.shape[1] // 2
        return whole[:, :height] / jnp.maximum(whole[:, height:], 1.0)

    lower = lower_warp(aims, first, second, second_maps, column_maps, groups)
    inner, outer = coadd(upper), coadd(lower)
    return jnp.concatenate([outer[:, :BEGIN], inner, outer[:, BEGIN:]], axis=1)


def solution(mesh):
    return jax.shard_map(
        local,
        mesh=mesh,
        in_specs=(
            P("visit", "sky", None),
            P("visit", "sky", None),
            P("visit", "sky", None),
            P("visit", None, None),
            P("visit", "sky", None),
            P("visit", "sky", None, None),
            P("visit", "sky", None, None, None),
            P("visit", "sky", None, None, None),
        ),
        out_specs=P(("visit", "sky"), None, None),
        check_vma=False,
    )
```

```python
import functools
import math

import jax
import jax.numpy as jnp
from jax import lax
from jax.experimental import pallas as pl
from jax.experimental.pallas import tpu as pltpu
from jax.sharding import PartitionSpec as P

BS = 128
HALO = 16
BAND = 16
CAP = 2
PB_DEV = 8
FROM, TO = 16, 96
CUT = TO - FROM
BEGIN, END = FROM + 8, TO - 8
EDGE = END - BEGIN
REACH = 16
FACTS = 8
FILTER_COLUMNS = 2048
UPPER_PARTS = 8
FILTER_VMEM = 60 * 1024 * 1024
UPPER_VMEM = 60 * 1024 * 1024
LOWER_VMEM = 58 * 1024 * 1024
LOWER_PARTS = 4


def toeplitz(rows, columns, shift, tap):
    lag = lax.broadcasted_iota(jnp.int32, (rows, columns), 0) - lax.broadcasted_iota(jnp.int32, (rows, columns), 1) + shift
    matrix = jnp.zeros((rows, columns), jnp.float32)
    for index, value in enumerate(tap):
        matrix = jnp.where(lag == index, value, matrix)
    return matrix.astype(jnp.bfloat16)

def segments(spans, rows):
    result, at, frame = [], 0, 0
    for first, last in spans:
        own_from, own_to = max(first - HALO, 0), min(last + HALO, rows)
        own_at = frame + own_from - (first - HALO)
        result.append((first, last, at, frame, own_from, own_to, own_at))
        at += last - first
        frame += last - first + 2 * HALO
    return result, at, frame


def filter_kernel(spans, owners, halo_count, owner_ref, taps_ref, *refs):
    exposure_ref, variance_ref, mask_ref = refs[:3]
    halo_refs = refs[3 : 3 + halo_count]
    pair_refs, out = refs[3 + halo_count : -15], refs[-15]
    framed, usable_ref, across_ref, down_ref, staged, facts_ref, known_ref, told_ref = refs[-14:-6]
    slot_ref, count_ref, here, near, done, cleared = refs[-6:]
    rows, columns = mask_ref.shape
    parted, height, tall = segments(spans, rows)
    wide = 2 * BS
    half = (taps_ref.shape[-1] - 1) // 2
    parts = here.shape[1]
    part_columns = columns // parts

    def fetched(part):
        lanes = pl.ds(part * part_columns, part_columns)
        inner = pl.ds(BS + part * part_columns, part_columns)
        pieces = []
        for first, last, at, _, own_from, own_to, own_at in parted:
            own, placed = pl.ds(own_from, own_to - own_from), pl.ds(own_at, own_to - own_from)
            kept, put = pl.ds(first, last - first), pl.ds(at, last - first)
            pieces += [
                (exposure_ref.at[own, lanes], framed.at[0, placed, inner]),
                (variance_ref.at[own, lanes], framed.at[1, placed, inner]),
                (mask_ref.at[kept, lanes], usable_ref.at[put, lanes]),
            ]
        return [
            pltpu.make_async_copy(source, target, here.at[index, part])
            for index, (source, target) in enumerate(pieces)
        ]

    halo_places = (0, tall - HALO)
    halos = [
        pltpu.make_async_copy(
            halo_ref.at[plane],
            framed.at[plane, pl.ds(place, HALO), pl.ds(BS, columns)],
            near.at[index, plane],
        )
        for index, (halo_ref, place) in enumerate(zip(halo_refs, halo_places))
        for plane in range(2)
    ]
    for copy in halos:
        copy.start()
    for part in range(parts):
        for copy in fetched(part):
            copy.start()

    for owner in range(count_ref.shape[0]):
        count_ref[owner] = 0
    for block in range(slot_ref.shape[0]):
        owner = owner_ref[0, 0, block]
        rank = count_ref[owner]
        slot_ref[block] = owner * CAP + rank
        count_ref[owner] = rank + 1

    sent = []
    if pair_refs:
        stretch_ref, offset_ref, patch_ref = pair_refs
        pairs, blocks = patch_ref.shape
        facts_ref[...] = jnp.ones(facts_ref.shape, jnp.float32)
        for pair in range(pairs):
            for base, ref in ((0, stretch_ref), (2 * pairs, offset_ref)):
                facts_ref[base + 2 * pair : base + 2 * pair + 2, :blocks] = ref[pair].astype(
                    jnp.float32
                )
        facts_ref[4 * pairs : 5 * pairs, :blocks] = patch_ref[...].astype(jnp.float32)
        facts_ref[...] = facts_ref[...].T
        known_ref[...] = jnp.zeros(known_ref.shape, jnp.float32)
        for block in range(blocks):
            slot = slot_ref[block]
            begin = pl.multiple_of((slot % CAP) * FACTS, FACTS)
            known_ref[slot // CAP, pl.ds(begin, FACTS), :] = jnp.broadcast_to(
                facts_ref[block : block + 1, :], (FACTS, BS)
            )
        told_ref[...] = known_ref[...].astype(jnp.bfloat16)
        tell = pltpu.make_async_copy(
            told_ref, out.at[:, pl.ds(2 * CAP * height, CAP * FACTS), :], cleared.at[0]
        )
        tell.start()
        sent.append(tell)

    margin = jnp.zeros((tall, BS), jnp.bfloat16)
    empty = jnp.zeros((BS, BS), jnp.bfloat16)
    values = taps_ref[0].astype(jnp.float32)
    for plane in range(2):
        framed[plane, :, :BS] = margin
        framed[plane, :, BS + columns :] = margin
        taps = [
            [values[way : way + 1, tap : tap + 1] for tap in range(taps_ref.shape[-1])]
            for way in range(2)
        ]
        if plane == 1:
            taps = [[tap * tap for tap in way] for way in taps]
        left, middle, right = (toeplitz(BS, BS, half + by * BS, taps[0]) for by in (-1, 0, 1))
        pattern = ((left, empty), (middle, left), (right, middle), (empty, right))
        for row, blocks in enumerate(pattern):
            across_ref[plane, row * BS : (row + 1) * BS, :BS] = blocks[0]
            across_ref[plane, row * BS : (row + 1) * BS, BS:] = blocks[1]
        place = lax.broadcasted_iota(jnp.int32, (height, tall), 0)
        shift = jnp.full((height, tall), half + HALO, jnp.int32)
        for _, _, at, frame, *_ in parted[1:]:
            shift = jnp.where(place >= at, half + HALO + frame - at, shift)
        down_ref[plane] = toeplitz(height, tall, shift, taps[1][::-1])

    for copy in halos:
        copy.wait()
    for place, outermost in list(zip(halo_places, (0, owners - 1)))[:halo_count]:
        inner = lax.axis_index("sky") != outermost
        for plane in range(2):
            halo = framed[plane, place : place + HALO, :]
            framed[plane, place : place + HALO, :] = jnp.where(inner, halo, jnp.zeros_like(halo))
    for copy in fetched(0):
        copy.wait()
    tiles = part_columns // wide
    for part in range(parts):
        if part + 1 < parts:
            for copy in fetched(part + 1):
                copy.wait()
        base = part * part_columns
        matched = []
        for plane in range(2):
            stack = jnp.concatenate(
                [
                    framed[plane, :, base + tile * wide : base + tile * wide + 4 * BS]
                    for tile in range(tiles)
                ],
                axis=0,
            )
            passed = jnp.dot(
                stack, across_ref[plane], preferred_element_type=jnp.float32
            ).astype(jnp.bfloat16)
            matched.append(
                [
                    jnp.dot(
                        down_ref[plane],
                        passed[tile * tall : (tile + 1) * tall],
                        preferred_element_type=jnp.float32,
                    )
                    for tile in range(tiles)
                ]
            )
        for tile in range(tiles):
            lanes = slice(base + tile * wide, base + (tile + 1) * wide)
            weight = usable_ref[:, lanes].astype(jnp.float32) / matched[1][tile]
            weighted = (weight * matched[0][tile]).astype(jnp.bfloat16)
            weight = weight.astype(jnp.bfloat16)
            for block in range(2):
                index = (part * tiles + tile) * 2 + block
                lanes = slice(block * BS, (block + 1) * BS)
                staged[index, :height, :] = weighted[:, lanes]
                staged[index, height : 2 * height, :] = weight[:, lanes]
        for index in range(part * tiles * 2, (part + 1) * tiles * 2):
            copy = pltpu.make_async_copy(
                staged.at[index],
                out.at[
                    slot_ref[index] // CAP,
                    pl.ds(pl.multiple_of((slot_ref[index] % CAP) * 2 * height, HALO), 2 * height),
                    :,
                ],
                done.at[index],
            )
            copy.start()
            sent.append(copy)
    for copy in sent:
        copy.wait()


def filtered(spans, owners, owner, taps, images, halos=(), facts=()):
    rows, columns = images[2].shape
    _, height, frame = segments(spans, rows)
    tall = CAP * (2 * height + (FACTS if facts else 0))
    blocks = columns // BS
    parts = columns // FILTER_COLUMNS
    smem = pl.BlockSpec(memory_space=pltpu.SMEM)
    hbm = pl.BlockSpec(memory_space=pltpu.HBM)

    def whole(array):
        return pl.BlockSpec(array.shape, lambda i: (0,) * array.ndim)

    operands = [owner, taps, *images, *halos, *facts]
    specs = [smem, whole(taps), hbm, hbm, hbm] + [pl.BlockSpec(memory_space=pl.ANY)] * len(halos)
    specs += [whole(fact) for fact in facts]
    return pl.pallas_call(
        functools.partial(filter_kernel, spans, owners, len(halos)),
        grid=(1,),
        out_shape=jax.ShapeDtypeStruct((owners, tall, BS), jnp.bfloat16),
        in_specs=specs,
        out_specs=hbm,
        scratch_shapes=[
            pltpu.VMEM((2, frame, columns + 2 * BS), jnp.bfloat16),
            pltpu.VMEM((height, columns), jnp.int32),
            pltpu.VMEM((2, 4 * BS, 2 * BS), jnp.bfloat16),
            pltpu.VMEM((2, height, frame), jnp.bfloat16),
            pltpu.VMEM((blocks, 2 * height, BS), jnp.bfloat16),
            pltpu.VMEM((BS, BS), jnp.float32),
            pltpu.VMEM((owners, CAP * FACTS, BS), jnp.float32),
            pltpu.VMEM((owners, CAP * FACTS, BS), jnp.bfloat16),
            pltpu.SMEM((blocks,), jnp.int32),
            pltpu.SMEM((owners,), jnp.int32),
            pltpu.SemaphoreType.DMA((3 * len(spans), parts)),
            pltpu.SemaphoreType.DMA((2, 2)),
            pltpu.SemaphoreType.DMA((blocks,)),
            pltpu.SemaphoreType.DMA((1,)),
        ],
        compiler_params=pltpu.CompilerParams(vmem_limit_bytes=FILTER_VMEM),
        cost_estimate=pl.CostEstimate(
            flops=2 * 10**9, bytes_accessed=16 * 2**20, transcendentals=0
        ),
        name="filter",
    )(*operands)


def series(square, count, odd):
    total = jnp.zeros_like(square)
    for term in range(count, -1, -1):
        total = total * square + (-1.0) ** term / math.factorial(2 * term + odd)
    return total


def accumulate(total, aims, rows, source, columns):
    height = rows.shape[0] // len(columns)
    half_warp = jnp.dot(rows, source, preferred_element_type=jnp.float32).astype(jnp.bfloat16)
    for pair, column in enumerate(columns):
        mine = half_warp[pair * height : (pair + 1) * height]
        both = jnp.concatenate([mine[:, :BS], mine[:, BS:]], axis=0)
        total[aims[pair]] += jnp.dot(both, column, preferred_element_type=jnp.float32)


def upper_kernel(pairs, aim_ref, table_ref, first_ref, second_out, column_out, *refs):
    outs, (block_ref, second_ref, column_ref, arrived, left) = refs[:-10], refs[-10:-5]
    total, spread_ref, place_ref, near_ref, taps_ref = refs[-5:]
    parts = arrived.shape[1]
    half = table_ref.shape[0] // 2
    per_part = half // parts
    lanes = lax.broadcasted_iota(jnp.int32, (BS, BS), 1)
    rows = lax.broadcasted_iota(jnp.int32, (BS, BS), 0)
    group = lanes // BAND
    centre = (BS - 1) / 2.0

    def fetched(part):
        return [
            pltpu.make_async_copy(
                first_ref.at[
                    pl.ds((base + part * per_part) // CAP, per_part // CAP),
                    pl.ds(0, 2 * CAP * CUT),
                    :,
                ],
                block_ref.at[pl.ds((base + part * per_part) // CAP, per_part // CAP)],
                arrived.at[index, part],
            )
            for index, base in enumerate((0, half))
        ]

    def returned(part):
        return [
            pltpu.make_async_copy(
                kept.at[pl.ds(base + part * per_part, per_part)],
                out.at[pl.ds(base + part * per_part, per_part)],
                left.at[2 * kind + index, part],
            )
            for index, base in enumerate((0, half))
            for kind, (kept, out) in enumerate(((second_ref, second_out), (column_ref, column_out)))
        ]

    for part in range(parts):
        for copy in fetched(part):
            copy.start()
    total[...] = jnp.zeros_like(total)
    target = rows + lanes % BAND - BAND // 2
    inside = (target >= 0) & (target < BS)
    place_ref[0] = rows.astype(jnp.float32) - centre
    place_ref[1] = jnp.where(inside, target.astype(jnp.float32) - centre, 1e3)

    facts = table_ref[...].astype(jnp.bfloat16)

    def sent(values, chosen):
        return jnp.dot(values, chosen.astype(jnp.bfloat16), preferred_element_type=jnp.float32)

    for kind in range(2):
        field = 2 * pairs * kind
        spread_ref[kind] = sent(
            facts[:half], (rows == field + 2 * group) & (group < pairs)
        ) + sent(facts[half:], (rows == field + 2 * (group - pairs)) & (group >= pairs))
    pixels = lanes[: 2 * half].astype(jnp.float32) - centre
    for pair in range(pairs):
        stretch = sent(facts, rows == 2 * pair + 1)
        offset = sent(facts, rows == 2 * pairs + 2 * pair + 1)
        source = (1.0 + stretch) * pixels + centre + offset
        near = jnp.round(source)
        x = source - near
        near_ref[pair] = near
        whole, third = math.pi * x, (math.pi / 3.0) * x
        whole_sinc = series(whole * whole, 8, 1)
        third_sinc = series(third * third, 8, 1)
        third_cos = series(third * third, 8, 0)
        for k in range(-3, 4):
            if k == 0:
                value = whole_sinc * third_sinc
            else:
                angle = math.pi * k / 3.0
                slow = third_sinc * third * math.cos(angle) - third_cos * math.sin(angle)
                far = x - k
                value = ((-1.0) ** k * 3.0 / math.pi**2) * whole_sinc * whole * slow / (far * far)
                value = jnp.where(jnp.abs(far) < 3.0, value, 0.0)
            taps_ref[k + 3, pair] = value

    numbers = rows.astype(jnp.bfloat16)

    def build(owner, rank):
        m = owner * CAP + rank
        stretch = spread_ref[0, pl.ds(m, 1), :]
        offset = spread_ref[1, pl.ds(m, 1), :]
        x = (1.0 + stretch) * place_ref[0] + offset - place_ref[1]
        square = x * x * (math.pi / 3.0) ** 2
        power = series(square, 10, 1)
        power = power * power
        value = power * (1.0 - (4.0 / 3.0) * power * square)
        value = jnp.where(jnp.abs(x) < 3.0, value, 0.0)
        for which in range(2):
            slot = m + which * half
            stack, columns = [], []
            for pair in range(pairs):
                index = which * pairs + pair
                one = jnp.where(group == index, value, 0.0)
                shift = -BAND // 2 - BAND * index
                inner, above, below = (
                    pltpu.roll(
                        one[begin:end], (shift + begin - lane) % BS, 1, stride=1, stride_axis=0
                    )
                    for begin, end, lane in (
                        (BEGIN, END, FROM),
                        (0, BEGIN, 0),
                        (END, BS, TO - FROM - 2 * REACH),
                    )
                )
                second_ref[slot, pair] = jnp.concatenate([above, below], axis=0).astype(
                    jnp.bfloat16
                )
                stack.append(inner.astype(jnp.bfloat16)[:, :CUT])
                lag = numbers - near_ref[pair, pl.ds(slot, 1), :].astype(jnp.bfloat16)
                column = jnp.zeros((BS, BS), jnp.bfloat16)
                for k in range(7):
                    tap = taps_ref[k, pair, pl.ds(slot, 1), :].astype(jnp.bfloat16)
                    column = jnp.where(lag == jnp.bfloat16(k - 3), tap, column)
                column_ref[slot, pair] = column
                columns.append(column)
            holder, base = owner + which * (half // CAP), rank * 2 * CUT
            source = jnp.concatenate(
                [
                    block_ref[holder, base : base + CUT, :],
                    block_ref[holder, base + CUT : base + 2 * CUT, :],
                ],
                axis=1,
            )
            aims = [aim_ref[slot * pairs + pair] for pair in range(pairs)]
            accumulate(total, aims, jnp.concatenate(stack, axis=0), source, columns)

    @pl.loop(0, parts)
    def _(part):
        for copy in fetched(part):
            copy.wait()

        @pl.loop(0, per_part // CAP)
        def _(owner):
            for rank in range(CAP):
                build(part * (per_part // CAP) + owner, rank)

        for copy in returned(part):
            copy.start()

    for index, out in enumerate(outs):
        out[...] = total[index * PB_DEV : (index + 1) * PB_DEV].astype(out.dtype)
    for part in range(parts):
        for copy in returned(part):
            copy.wait()


def upper_warp(aims, table, first, pairs, groups):
    slots = first.shape[0] * CAP
    second = jax.ShapeDtypeStruct((slots, pairs, BS - EDGE, BS), jnp.bfloat16)
    column = jax.ShapeDtypeStruct((slots, pairs, BS, BS), jnp.bfloat16)
    hbm = pl.BlockSpec(memory_space=pltpu.HBM)
    return pl.pallas_call(
        functools.partial(upper_kernel, pairs),
        grid=(1,),
        in_specs=[
            pl.BlockSpec(memory_space=pltpu.SMEM),
            pl.BlockSpec(table.shape, lambda i: (0, 0)),
            pl.BlockSpec(memory_space=pl.ANY),
        ],
        out_specs=[hbm, hbm]
        + [pl.BlockSpec((PB_DEV, 2 * EDGE, BS), lambda i: (0, 0, 0))] * groups,
        scratch_shapes=[
            pltpu.VMEM((slots // CAP, 2 * CAP * CUT, BS), jnp.bfloat16),
            pltpu.VMEM(second.shape, second.dtype),
            pltpu.VMEM(column.shape, column.dtype),
            pltpu.SemaphoreType.DMA((2, UPPER_PARTS)),
            pltpu.SemaphoreType.DMA((4, UPPER_PARTS)),
            pltpu.VMEM((groups * PB_DEV + 1, 2 * EDGE, BS), jnp.float32),
            pltpu.VMEM((2, slots // 2, BS), jnp.float32),
            pltpu.VMEM((2, BS, BS), jnp.float32),
            pltpu.VMEM((pairs, slots, BS), jnp.float32),
            pltpu.VMEM((7, pairs, slots, BS), jnp.float32),
        ],
        out_shape=[second, column]
        + [
            jax.ShapeDtypeStruct(
                (PB_DEV, 2 * EDGE, BS), jnp.float32 if index == 0 else jnp.bfloat16
            )
            for index in range(groups)
        ],
        compiler_params=pltpu.CompilerParams(vmem_limit_bytes=UPPER_VMEM),
        cost_estimate=pl.CostEstimate(
            flops=10**10, bytes_accessed=32 * 2**20, transcendentals=0
        ),
        name="upper_warp",
    )(aims, table, first)


def lower_kernel(pairs, aim_ref, *refs):
    (first, second, row, column), outs = refs[:4], refs[4:-6]
    first_ref, second_ref, row_ref, column_ref, total, arrived = refs[-6:]
    parts = arrived.shape[1]
    per_part = row_ref.shape[0] // parts
    far = BS - CUT

    def copies(part):
        slots = pl.ds(part * per_part, per_part)
        holders = pl.ds(part * per_part // CAP, per_part // CAP)
        pieces = [
            (
                first.at[holders, pl.ds(rank * 2 * CUT + begin, count), :],
                first_ref.at[holders, pl.ds(rank * 4 * REACH + place, count), :],
            )
            for rank in range(CAP)
            for begin, count, place in (
                (0, REACH, 0),
                (CUT - REACH, 2 * REACH, REACH),
                (2 * CUT - REACH, REACH, 3 * REACH),
            )
        ]
        pieces += [
            (second.at[holders], second_ref.at[holders]),
            (row.at[slots], row_ref.at[slots]),
            (column.at[slots], column_ref.at[slots]),
        ]
        return [
            pltpu.make_async_copy(source, kept, arrived.at[index, part])
            for index, (source, kept) in enumerate(pieces)
        ]

    for part in range(parts):
        for copy in copies(part):
            copy.start()
    total[...] = jnp.zeros_like(total)

    @pl.loop(0, parts)
    def _(part):
        for copy in copies(part):
            copy.wait()
        for inner in range(per_part):
            slot = part * per_part + inner
            holder = part * (per_part // CAP) + inner // CAP
            near_at, far_at = (inner % CAP) * 4 * REACH, (inner % CAP) * 2 * far
            source = jnp.concatenate(
                [
                    jnp.concatenate(
                        [
                            second_ref[holder, begin : begin + FROM, :],
                            first_ref[holder, near : near + 2 * REACH, :],
                            second_ref[holder, begin + FROM : begin + far, :],
                        ],
                        axis=0,
                    )
                    for near, begin in (
                        (near_at, far_at),
                        (near_at + 2 * REACH, far_at + far),
                    )
                ],
                axis=1,
            )
            aims = [aim_ref[slot * pairs + pair] for pair in range(pairs)]
            rows = row_ref[slot].reshape(pairs * row_ref.shape[2], BS)[:, : 2 * REACH + far]
            columns = [column_ref[slot, pair] for pair in range(pairs)]
            accumulate(total, aims, rows, source, columns)

    for index, out in enumerate(outs):
        out[...] = total[index * PB_DEV : (index + 1) * PB_DEV].astype(out.dtype)


def lower_warp(aims, first, second, row_maps, column_maps, groups):
    slots, pairs, height, _ = row_maps.shape
    operands = [first, second, row_maps, column_maps]
    return pl.pallas_call(
        functools.partial(lower_kernel, pairs),
        in_specs=[pl.BlockSpec(memory_space=pltpu.SMEM)]
        + [pl.BlockSpec(memory_space=pl.ANY)] * len(operands),
        out_specs=[pl.BlockSpec(memory_space=pltpu.VMEM)] * groups,
        scratch_shapes=[
            pltpu.VMEM((slots // CAP, 4 * CAP * REACH, BS), first.dtype),
            pltpu.VMEM(second.shape, second.dtype),
            pltpu.VMEM(row_maps.shape, row_maps.dtype),
            pltpu.VMEM(column_maps.shape, column_maps.dtype),
            pltpu.VMEM((groups * PB_DEV + 1, 2 * height, BS), jnp.float32),
            pltpu.SemaphoreType.DMA((3 * CAP + 3, LOWER_PARTS)),
        ],
        out_shape=[
            jax.ShapeDtypeStruct(
                (PB_DEV, 2 * height, BS), jnp.float32 if index == 0 else jnp.bfloat16
            )
            for index in range(groups)
        ],
        compiler_params=pltpu.CompilerParams(vmem_limit_bytes=LOWER_VMEM),
        cost_estimate=pl.CostEstimate(
            flops=6 * 10**9, bytes_accessed=32 * 2**20, transcendentals=0
        ),
        name="lower_warp",
    )(aims, *operands)


def local(
    exposure, variance, pixel_mask, psf_kernel, block_owner, patch_index, pair_stretch, pair_offset
):
    _, rows, columns = exposure.shape
    block_count = columns // BS
    owners = lax.axis_size("sky")
    groups = lax.axis_size("visit")
    slots = owners * CAP
    pairs = patch_index.shape[-1]

    def exchange(array):
        return lax.all_to_all(array, "sky", split_axis=0, concat_axis=0, tiled=True)

    low = jnp.concatenate([exposure[:, rows - HALO :], variance[:, rows - HALO :]], axis=0)
    high = jnp.concatenate([exposure[:, :HALO], variance[:, :HALO]], axis=0)
    even = lax.axis_index("sky") % 2 == 0
    near = lax.ppermute(
        jnp.where(even, low, high), "sky", [(i, i ^ 1) for i in range(owners)]
    )
    far = lax.ppermute(
        jnp.where(even, high, low),
        "sky",
        [(i, (i - 1 if i % 2 == 0 else i + 1) % owners) for i in range(owners)],
    )

    facts = [
        pair_stretch.transpose(0, 1, 3, 4, 2).reshape(pairs, 2, block_count),
        pair_offset.transpose(0, 1, 3, 4, 2).reshape(pairs, 2, block_count),
        patch_index.transpose(0, 1, 3, 2).reshape(pairs, block_count),
    ]

    images = [array.reshape(rows, columns) for array in (exposure, variance, pixel_mask)]
    common = (owners, block_owner, psf_kernel, images)
    inner_planes = filtered([(FROM, TO)], *common, facts=facts)
    inner_planes, near, far = lax.optimization_barrier((inner_planes, near, far))
    first = exchange(inner_planes)

    top, bottom = jnp.where(even, far, near), jnp.where(even, near, far)
    outer_planes = filtered([(0, FROM), (TO, rows)], *common, halos=(top, bottom))
    first, outer_planes = lax.optimization_barrier((first, outer_planes))
    second = exchange(outer_planes)

    table = first[:, 2 * CAP * CUT :: FACTS, :].astype(jnp.float32).reshape(slots, BS)
    patch = table[:, 4 * pairs : 5 * pairs].astype(jnp.int32)
    distance = (patch // PB_DEV) ^ lax.axis_index("visit")
    aims = jnp.where(
        table[:, 5 * pairs : 5 * pairs + 1] > 0.5,
        distance * PB_DEV + patch % PB_DEV,
        groups * PB_DEV,
    )
    aims = aims.reshape(slots * pairs)
    second_maps, column_maps, *upper = upper_warp(aims, table, first, pairs, groups)

    def coadd(sums):
        whole = sums[0]
        for step in (2, 1, 3):
            ring = [(i, i ^ step) for i in range(groups)]
            whole = whole + lax.ppermute(sums[step], "visit", ring).astype(jnp.float32)
        height = whole.shape[1] // 2
        return whole[:, :height] / jnp.maximum(whole[:, height:], 1.0)

    lower = lower_warp(aims, first, second, second_maps, column_maps, groups)
    inner, outer = coadd(upper), coadd(lower)
    return jnp.concatenate([outer[:, :BEGIN], inner, outer[:, BEGIN:]], axis=1)


def solution(mesh):
    return jax.shard_map(
        local,
        mesh=mesh,
        in_specs=(
            P("visit", "sky", None),
            P("visit", "sky", None),
            P("visit", "sky", None),
            P("visit", None, None),
            P("visit", "sky", None),
            P("visit", "sky", None, None),
            P("visit", "sky", None, None, None),
            P("visit", "sky", None, None, None),
        ),
        out_specs=P(("visit", "sky"), None, None),
        check_vma=False,
    )
```
